512 devices in a mesh: seq: 64 (over z, x, core), chan: 8 (over y).
Axes of the slice: x: 4, y: 8, z: 8, core: 2. Of those that a mesh axis runs over, the one named last changes fastest.
Arguments:
- gate_input: bfloat16 [4096, 4096], P('seq', 'chan'), may hold values from -6 to 6
- key_input: bfloat16 [4096, 4096], P('seq', 'chan'), may hold values from -6 to 6
- value_input: bfloat16 [4096, 4096], P('seq', 'chan'), may hold values from -6 to 6
- decay_rate: float32 [16, 4096], P(None, 'chan'), may hold values from 0.00024414062 to 0.1
- residue: float32 [16, 4096], P(None, 'chan'), may hold values from -1.5 to 1.5
- skip_gain: float32 [4096], P('chan'), may hold values from -3 to 3
- out_weight: bfloat16 [4096, 4096], P('chan', 'seq'), may hold values from -0.25 to 0.25
Outputs:
- mixed: bfloat16 [4096, 4096], P('seq', 'chan')
The draws below stay inside these ranges and needn't reach their ends.
All inputs are finite; a program needn't handle non-finite values.
Results may differ from the reference program's by a relative error of at most 0.014.
Values may be sent and summed in bfloat16 or wider, within the bound.
No kernel may reach another device: no remote copies, remote signals or barrier semaphores. Data moves between devices by JAX's collectives and lax.ppermute only.
A program may use at most 64 MiB of HBM per device.

```python
import math
import jax
import jax.numpy as jnp
from jax import lax

D = 4096
MODES = 16
TOK_DEV = 64
LENGTH = 4096
N_SEQ = 64
N_CHAN = 8


def strengthened(array, own_key, source, target, blocks, factor):
    owner, partner = [(jnp.arange(array.shape[dim]) // (array.shape[dim] // blocks)).reshape([-1 if axis == dim else 1 for axis in range(array.ndim)]) for dim in (source, target)]
    chosen = jax.random.permutation(own_key, blocks)[partner]
    strong = (owner == chosen) | (owner == (partner + blocks // 2) % blocks)
    return jnp.where(strong, factor * array, array)


def block_scale(rng, extent, split, smallest, top_value):
    loudness, own = 1.0, jax.random.fold_in(rng, 6)
    for dim, shards_of in split:
        steps = jnp.exp(jax.random.uniform(jax.random.fold_in(own, dim), (shards_of,), jnp.float32, smallest / len(split), top_value / len(split)))
        loudness = loudness * jnp.repeat(steps, extent[dim] // shards_of).reshape([-1 if axis == dim else 1 for axis in range(len(extent))])
    return loudness


def gaussian(rng, dims, width, most, shards=(), dtype=jnp.bfloat16):
    drawn = width * jax.random.normal(rng, dims, jnp.float32)
    if shards:
        drawn = drawn * block_scale(rng, dims, shards, -0.22, 0.18)
    return jnp.clip(drawn, -most, most).astype(dtype)


def gaussian_with(stream_key, dims, scale, reach, cuts, heavy, dtype=jnp.bfloat16):
    values = scale * jax.random.normal(stream_key, dims, jnp.float32)
    if cuts:
        values = values * block_scale(stream_key, dims, cuts, -0.22, 0.18)
    return jnp.clip(strengthened(values, jax.random.fold_in(stream_key, 3), *heavy), -reach, reach).astype(dtype)


def setup_inputs(seed: int = 0) -> dict:
    splits = jax.random.split(jax.random.key(seed), 8)
    return {
        "gate_input": gaussian(splits[0], (LENGTH, D), 1.0, 6.0, ((0, 64), (1, 8))),
        "key_input": gaussian(splits[1], (LENGTH, D), 1.0, 6.0, ((0, 64), (1, 8))),
        "value_input": gaussian(splits[2], (LENGTH, D), 1.0, 6.0, ((0, 64), (1, 8))),
        "decay_rate": jnp.clip(jnp.exp(math.log(0.1) - 6.015181 * jax.random.uniform(splits[3], (MODES, D), jnp.float32) ** block_scale(splits[3], (MODES, D), ((1, 8),), -0.2, 0.2)), 0.00024414062, 0.1),
        "residue": gaussian(splits[4], (MODES, D), MODES ** -0.5, 1.5, ((1, 8),), jnp.float32),
        "skip_gain": gaussian(splits[5], (D,), 0.5, 3.0, ((0, 8),), jnp.float32),
        "out_weight": gaussian_with(splits[6], (D, D), D ** -0.5, 0.25, ((0, 8), (1, 64)), (0, 1, 64, 4.0)),
    }


def reference(gate_input, key_input, value_input, decay_rate, residue, skip_gain, out_weight):
    total_rows = TOK_DEV * N_SEQ
    padded_len = 2 * total_rows
    group_cols = D // N_CHAN
    signal = key_input.astype(jnp.float32) * value_input.astype(jnp.float32)
    amplitude = residue * jnp.sqrt(-jnp.expm1(-2.0 * decay_rate))
    positions = jnp.arange(total_rows).astype(jnp.float32)
    pieces = []
    for group_index in range(N_CHAN):
        first_col = group_index * group_cols
        group_signal = signal[:, first_col:first_col + group_cols]
        rates = decay_rate[:, first_col:first_col + group_cols]
        amps = amplitude[:, first_col:first_col + group_cols]

        def add_mode(mode_index, totals):
            return totals + amps[mode_index][None, :] * jnp.exp(-rates[mode_index][None, :] * positions[:, None])
        response = lax.fori_loop(0, MODES, add_mode, jnp.zeros((total_rows, group_cols), jnp.float32))
        product = jnp.fft.rfft(group_signal, n=padded_len, axis=0) * jnp.fft.rfft(response, n=padded_len, axis=0)
        pieces.append(jnp.fft.irfft(product, n=padded_len, axis=0)[:total_rows])
    convolved = jnp.concatenate(pieces, axis=1)
    gated_rows = (gate_input.astype(jnp.float32) * (convolved + skip_gain[None, :] * signal)).astype(jnp.bfloat16)
    summed = jnp.zeros((total_rows, D), jnp.float32)
    for group_index in range(N_CHAN):
        first_col = group_index * group_cols
        partial_sum = jnp.dot(gated_rows[:, first_col:first_col + group_cols].astype(jnp.float32), out_weight[first_col:first_col + group_cols].astype(jnp.float32), precision=lax.Precision.HIGHEST)
        summed = summed + partial_sum.astype(jnp.bfloat16).astype(jnp.float32)
    return summed.astype(jnp.bfloat16)
```

```python
import jax
import jax.numpy as jnp
from jax import lax
from jax.experimental import pallas as pl
from jax.experimental.pallas import tpu as pltpu
from jax.sharding import Mesh
from jax.sharding import PartitionSpec as P

F32 = jnp.float32
BF16 = jnp.bfloat16
SEQ = ("z", "x", "core")
LANES = 128
VMEM = pl.BlockSpec(memory_space=pltpu.VMEM)
SMEM = pl.BlockSpec(memory_space=pltpu.SMEM)
PARAMS = pltpu.CompilerParams(vmem_limit_bytes=48 * 1024 * 1024)


def tile_rows():
    return lax.broadcasted_iota(jnp.int32, (8, LANES), 0).astype(F32)


def own_rows_kernel(key_ref, value_ref, rate_ref, amp_ref, skip_ref, base_ref, state_ref):
    rows, width = key_ref.shape
    modes = rate_ref.shape[0]
    tiles = rows // 8
    copies = state_ref.shape[0]

    def slab(index, carry):
        cols = pl.ds(pl.multiple_of(index * LANES, LANES), LANES)
        signal = key_ref[:, cols].astype(F32) * value_ref[:, cols].astype(F32)
        rate = rate_ref[:, cols]
        amp = amp_ref[:, cols]
        steps = [jnp.exp(-8.0 * j * rate) for j in range(tiles)]
        scaled = [amp * step for step in steps]
        first = tile_rows()
        taps = [jnp.zeros((8, LANES), F32) for _ in range(tiles)]
        states = []
        for m in range(modes):
            ahead = jnp.exp(-rate[m : m + 1] * first)
            behind = jnp.exp(-rate[m : m + 1] * (7.0 - first))
            held = jnp.zeros((8, LANES), F32)
            for j in range(tiles):
                taps[j] = taps[j] + scaled[j][m : m + 1] * ahead
                held = held + steps[tiles - 1 - j][m : m + 1] * signal[8 * j : 8 * j + 8]
            states.append(jnp.sum(held * behind, axis=0, keepdims=True))
        state = jnp.concatenate(states, axis=0)
        for copy in range(copies):
            state_ref[copy, :, cols] = state
        row_ids = lax.broadcasted_iota(jnp.int32, (rows, LANES), 0)
        totals = [
            skip_ref[0:1, cols] * signal[8 * j : 8 * j + 8] for j in range(tiles)
        ]
        for lag in range(8):
            moved = signal
            if lag:
                moved = jnp.where(row_ids >= lag, pltpu.roll(signal, lag, 0), 0.0)
            for j in range(tiles):
                tap = taps[j][lag : lag + 1]
                for i in range(j, tiles):
                    totals[i] = totals[i] + tap * moved[8 * (i - j) : 8 * (i - j) + 8]
        for j in range(tiles):
            base_ref[8 * j : 8 * j + 8, cols] = totals[j]
        return carry

    lax.fori_loop(0, width // LANES, slab, 0)


def row_block_kernel(rows, where_ref, states_ref, rate_ref, before_ref, total_ref):
    own = where_ref[0]
    decay = jnp.exp(-float(rows) * rate_ref[...])
    running = jnp.zeros(rate_ref.shape, F32)
    before = jnp.zeros(rate_ref.shape, F32)
    for j in range(states_ref.shape[0]):
        before = jnp.where(own == j, running, before)
        running = decay * running + states_ref[j]
    before_ref[...] = before
    for copy in range(total_ref.shape[0]):
        total_ref[copy] = running


def gate_kernel(
    rows, where_ref, totals_ref, before_ref, rate_ref, amp_ref, base_ref, gate_ref, gated_ref
):
    own = where_ref[0].astype(F32)
    block = where_ref[1]
    blocks, modes, width = totals_ref.shape
    tiles = rows // 8

    def slab(index, carry):
        cols = pl.ds(pl.multiple_of(index * LANES, LANES), LANES)
        rate = rate_ref[:, cols]
        decay = jnp.exp(-float(rows * 8) * rate)
        running = jnp.zeros((modes, LANES), F32)
        entering = jnp.zeros((modes, LANES), F32)
        for z in range(blocks):
            entering = jnp.where(block == z, running, entering)
            running = decay * running + totals_ref[z, :, cols]
        state = before_ref[:, cols] + jnp.exp(-float(rows) * own * rate) * entering
        state = state * amp_ref[:, cols]
        scaled = [state * jnp.exp(-8.0 * j * rate) for j in range(tiles)]
        first = tile_rows() + 1.0
        totals = [base_ref[8 * j : 8 * j + 8, cols] for j in range(tiles)]
        for m in range(modes):
            ahead = jnp.exp(-rate[m : m + 1] * first)
            for j in range(tiles):
                totals[j] = totals[j] + scaled[j][m : m + 1] * ahead
        result = jnp.concatenate(totals, axis=0)
        gated_ref[:, cols] = (gate_ref[:, cols].astype(F32) * result).astype(BF16)
        return carry

    lax.fori_loop(0, width // LANES, slab, 0)


def project_kernel(gated_ref, weight_ref, out_ref):
    cores, rows, depth = gated_ref.shape
    gated = gated_ref[...].reshape(cores * rows, depth)
    weight = weight_ref[...].reshape(-1, depth)
    part = lax.dot_general(
        gated, weight, (((1,), (1,)), ((), ())), preferred_element_type=F32
    ).astype(BF16)
    out_ref[...] = part.reshape(out_ref.shape)


def sum_kernel(parts_ref, out_ref):
    groups, cores, rows, width = parts_ref.shape
    unit = out_ref.shape[1] // (width // 64 * cores)
    totals = []
    for core in range(cores):
        total = parts_ref[0, core].astype(F32)
        for j in range(1, groups):
            total = total + parts_ref[j, core].astype(F32)
        totals.append(total)
    pieces = []
    for j in range(width // unit):
        for core in range(cores):
            pieces.append(totals[core][:, j * unit : (j + 1) * unit])
    out_ref[...] = jnp.concatenate(pieces, axis=1).astype(BF16)


def exchange(x, axes):
    return lax.all_to_all(x, axes, 0, 0, tiled=True)


def body(gate_input, key_input, value_input, decay_rate, residue, skip_gain, out_weight):
    rows, width = key_input.shape
    modes = decay_rate.shape[0]
    z_size, x_size, y_size = (lax.axis_size(a) for a in ("z", "x", "chan"))
    cores = lax.axis_size("core")
    out_cols = out_weight.shape[1]
    where = jnp.stack([lax.axis_index(("x", "core")), lax.axis_index("z")]).astype(jnp.int32)

    own_weight = jnp.broadcast_to(out_weight.T[None], (z_size, out_cols, width))
    weight_z = exchange(own_weight, "z")
    weight = exchange(jnp.broadcast_to(weight_z[None], (x_size,) + weight_z.shape), "x")
    weight = weight.reshape(x_size, z_size, out_cols, width)

    amplitude = residue * jnp.sqrt(-jnp.expm1(-2.0 * decay_rate))
    base, states = pl.pallas_call(
        own_rows_kernel,
        out_shape=(
            jax.ShapeDtypeStruct((rows, width), F32),
            jax.ShapeDtypeStruct((x_size * cores, modes, width), F32),
        ),
        in_specs=[VMEM] * 5,
        out_specs=(VMEM, VMEM),
        compiler_params=PARAMS,
        name="own_rows",
    )(key_input, value_input, decay_rate, amplitude, skip_gain[None, :])
    states = exchange(states, ("x", "core"))
    before, total = pl.pallas_call(
        lambda *refs: row_block_kernel(rows, *refs),
        out_shape=(
            jax.ShapeDtypeStruct((modes, width), F32),
            jax.ShapeDtypeStruct((z_size, modes, width), F32),
        ),
        in_specs=[SMEM, VMEM, VMEM],
        out_specs=(VMEM, VMEM),
        compiler_params=PARAMS,
        name="row_block",
    )(where, states, decay_rate)
    totals = exchange(total, "z")
    gated = pl.pallas_call(
        lambda *refs: gate_kernel(rows, *refs),
        out_shape=jax.ShapeDtypeStruct((rows, width), BF16),
        in_specs=[SMEM] + [VMEM] * 6,
        out_specs=VMEM,
        compiler_params=PARAMS,
        name="gate",
    )(where, totals, before, decay_rate, amplitude, base, gate_input)
    gated = lax.all_gather(gated, "core")
    parts = pl.pallas_call(
        project_kernel,
        grid=(z_size,),
        out_shape=jax.ShapeDtypeStruct((y_size, cores, rows, x_size * out_cols), BF16),
        in_specs=[
            pl.BlockSpec((cores, rows, width), lambda i: (0, 0, 0)),
            pl.BlockSpec((x_size, 1, out_cols, width), lambda i: (0, i, 0, 0)),
        ],
        out_specs=pl.BlockSpec((1, cores, rows, x_size * out_cols), lambda i: (i, 0, 0, 0)),
        compiler_params=PARAMS,
        name="project",
    )(gated, weight)
    parts = parts.reshape(y_size * cores, rows, x_size * out_cols)
    parts = exchange(parts, ("chan", "core")).reshape(y_size, cores, rows, x_size * out_cols)
    return pl.pallas_call(
        sum_kernel,
        out_shape=jax.ShapeDtypeStruct((rows, width), BF16),
        in_specs=[VMEM],
        out_specs=VMEM,
        compiler_params=PARAMS,
        name="sum_parts",
    )(parts)


def solution(mesh):
    finer = Mesh(
        mesh.devices.reshape(8, 4, 2, mesh.shape["chan"]), ("z", "x", "core", "chan")
    )
    return jax.shard_map(
        body,
        mesh=finer,
        in_specs=(
            P(SEQ, "chan"),
            P(SEQ, "chan"),
            P(SEQ, "chan"),
            P(None, "chan"),
            P(None, "chan"),
            P("chan"),
            P("chan", SEQ),
        ),
        out_specs=P(SEQ, "chan"),
        check_vma=False,
    )
```

```python
import jax
import jax.numpy as jnp
from jax import lax
from jax.experimental import pallas as pl
from jax.experimental.pallas import tpu as pltpu
from jax.sharding import Mesh
from jax.sharding import PartitionSpec as P

F32 = jnp.float32
BF16 = jnp.bfloat16
SEQ = ("z", "x", "core")
LANES = 128
SHIFTS = (0, 1, 3, 2)
VMEM = pl.BlockSpec(memory_space=pltpu.VMEM)
SMEM = pl.BlockSpec(memory_space=pltpu.SMEM)
PARAMS = pltpu.CompilerParams(vmem_limit_bytes=48 * 1024 * 1024)


def tile_rows():
    return lax.broadcasted_iota(jnp.int32, (8, LANES), 0).astype(F32)


def own_rows_kernel(
    key_ref, value_ref, rate_ref, residue_ref, skip_ref, base_ref, state_ref, amp_ref, copy_ref
):
    rows, width = key_ref.shape
    modes = rate_ref.shape[0]
    tiles = rows // 8
    copies = state_ref.shape[0]

    def slab(index, carry):
        cols = pl.ds(pl.multiple_of(index * LANES, LANES), LANES)
        signal = key_ref[:, cols].astype(F32) * value_ref[:, cols].astype(F32)
        rate = rate_ref[:, cols]
        amp = residue_ref[:, cols] * jnp.sqrt(1.0 - jnp.exp(-2.0 * rate))
        amp_ref[:, cols] = amp
        copy_ref[:, cols] = rate
        steps = [jnp.exp(-8.0 * j * rate) for j in range(tiles)]
        scaled = [amp * step for step in steps]
        first = tile_rows()
        taps = [jnp.zeros((8, LANES), F32) for _ in range(tiles)]
        states = []
        for m in range(modes):
            ahead = jnp.exp(-rate[m : m + 1] * first)
            behind = jnp.exp(-rate[m : m + 1] * (7.0 - first))
            held = jnp.zeros((8, LANES), F32)
            for j in range(tiles):
                taps[j] = taps[j] + scaled[j][m : m + 1] * ahead
                held = held + steps[tiles - 1 - j][m : m + 1] * signal[8 * j : 8 * j + 8]
            states.append(jnp.sum(held * behind, axis=0, keepdims=True))
        state = jnp.concatenate(states, axis=0)
        for copy in range(copies):
            state_ref[copy, :, cols] = state
        row_ids = lax.broadcasted_iota(jnp.int32, (rows, LANES), 0)
        totals = [
            skip_ref[0:1, cols] * signal[8 * j : 8 * j + 8] for j in range(tiles)
        ]
        for lag in range(8):
            moved = signal
            if lag:
                moved = jnp.where(row_ids >= lag, pltpu.roll(signal, lag, 0), 0.0)
            for j in range(tiles):
                tap = taps[j][lag : lag + 1]
                for i in range(j, tiles):
                    totals[i] = totals[i] + tap * moved[8 * (i - j) : 8 * (i - j) + 8]
        for j in range(tiles):
            base_ref[8 * j : 8 * j + 8, cols] = totals[j]
        return carry

    lax.fori_loop(0, width // LANES, slab, 0)


def row_block_kernel(rows, where_ref, states_ref, rate_ref, before_ref, total_ref):
    own = where_ref[0]
    decay = jnp.exp(-float(rows) * rate_ref[...])
    running = jnp.zeros(rate_ref.shape, F32)
    before = jnp.zeros(rate_ref.shape, F32)
    for j in range(states_ref.shape[0]):
        before = jnp.where(own == j, running, before)
        running = decay * running + states_ref[j]
    before_ref[...] = before
    for copy in range(total_ref.shape[0]):
        total_ref[copy] = running


def gate_kernel(
    rows, where_ref, totals_ref, before_ref, rate_ref, amp_ref, base_ref, gate_ref, gated_ref
):
    own = where_ref[0].astype(F32)
    block = where_ref[1]
    blocks, modes, width = totals_ref.shape
    tiles = rows // 8

    def slab(index, carry):
        cols = pl.ds(pl.multiple_of(index * LANES, LANES), LANES)
        rate = rate_ref[:, cols]
        decay = jnp.exp(-float(rows * 8) * rate)
        running = jnp.zeros((modes, LANES), F32)
        entering = jnp.zeros((modes, LANES), F32)
        for z in range(blocks):
            entering = jnp.where(block == z, running, entering)
            running = decay * running + totals_ref[z, :, cols]
        state = before_ref[:, cols] + jnp.exp(-float(rows) * own * rate) * entering
        state = state * amp_ref[:, cols]
        scaled = [state * jnp.exp(-8.0 * j * rate) for j in range(tiles)]
        first = tile_rows() + 1.0
        totals = [base_ref[8 * j : 8 * j + 8, cols] for j in range(tiles)]
        for m in range(modes):
            ahead = jnp.exp(-rate[m : m + 1] * first)
            for j in range(tiles):
                totals[j] = totals[j] + scaled[j][m : m + 1] * ahead
        result = jnp.concatenate(totals, axis=0)
        gated_ref[:, cols] = (gate_ref[:, cols].astype(F32) * result).astype(BF16)
        return carry

    lax.fori_loop(0, width // LANES, slab, 0)


def project_kernel(gated_ref, *refs):
    weight_refs, out_ref = refs[:-1], refs[-1]
    cores, rows, depth = gated_ref.shape
    gated = gated_ref[...].reshape(cores * rows, depth)
    for j in range(out_ref.shape[0]):
        weight = jnp.concatenate([ref[j] for ref in weight_refs], axis=0)
        part = lax.dot_general(
            gated, weight, (((1,), (1,)), ((), ())), preferred_element_type=F32
        ).astype(BF16)
        out_ref[j] = part.reshape(out_ref.shape[1:])


def sum_kernel(where_ref, parts_ref, out_ref):
    groups, cores, rows, width = parts_ref.shape
    unit = out_ref.shape[1] // (len(SHIFTS) * cores)
    own_x = where_ref[2]
    totals = []
    for core in range(cores):
        total = parts_ref[0, core].astype(F32)
        for j in range(1, groups):
            total = total + parts_ref[j, core].astype(F32)
        totals.append(total)
    for j, shift in enumerate(SHIFTS):
        pieces = [total[:, j * unit : (j + 1) * unit] for total in totals]
        source = lax.rem(own_x + (len(SHIFTS) - shift), len(SHIFTS))
        place = pl.multiple_of(source * (cores * unit), cores * unit)
        out_ref[:, pl.ds(place, cores * unit)] = jnp.concatenate(pieces, axis=1).astype(BF16)


def exchange(x, axes):
    return lax.all_to_all(x, axes, 0, 0, tiled=True)


def body(gate_input, key_input, value_input, decay_rate, residue, skip_gain, out_weight):
    rows, width = key_input.shape
    modes = decay_rate.shape[0]
    z_size, x_size, y_size = (lax.axis_size(a) for a in ("z", "x", "chan"))
    cores = lax.axis_size("core")
    out_cols = out_weight.shape[1]
    where = jnp.stack(
        [lax.axis_index(("x", "core")), lax.axis_index("z"), lax.axis_index("x")]
    ).astype(jnp.int32)

    own_weight = jnp.broadcast_to(out_weight.T[None], (z_size, out_cols, width))
    weight_z = exchange(own_weight, "z")
    state_shape = jax.ShapeDtypeStruct((modes, width), F32)
    base, states, amplitude, rate = pl.pallas_call(
        own_rows_kernel,
        out_shape=(
            jax.ShapeDtypeStruct((rows, width), F32),
            jax.ShapeDtypeStruct((x_size * cores, modes, width), F32),
            state_shape,
            state_shape,
        ),
        in_specs=[VMEM] * 5,
        out_specs=(VMEM,) * 4,
        compiler_params=PARAMS,
        name="own_rows",
    )(key_input, value_input, decay_rate, residue, skip_gain[None, :])
    states, weight_z = lax.optimization_barrier((states, weight_z))
    weights = [weight_z] + [
        lax.ppermute(weight_z, "x", [(i, (i + shift) % x_size) for i in range(x_size)])
        for shift in SHIFTS[1:]
    ]
    states = exchange(states, ("x", "core"))
    before, total = pl.pallas_call(
        lambda *refs: row_block_kernel(rows, *refs),
        out_shape=(
            jax.ShapeDtypeStruct((modes, width), F32),
            jax.ShapeDtypeStruct((z_size, modes, width), F32),
        ),
        in_specs=[SMEM, VMEM, VMEM],
        out_specs=(VMEM, VMEM),
        compiler_params=PARAMS,
        name="row_block",
    )(where, states, rate)
    totals = exchange(total, "z")
    gated = pl.pallas_call(
        lambda *refs: gate_kernel(rows, *refs),
        out_shape=jax.ShapeDtypeStruct((rows, width), BF16),
        in_specs=[SMEM] + [VMEM] * 6,
        out_specs=VMEM,
        compiler_params=PARAMS,
        name="gate",
    )(where, totals, before, rate, amplitude, base, gate_input)
    gated = lax.all_gather(gated, "core")
    parts = pl.pallas_call(
        project_kernel,
        out_shape=jax.ShapeDtypeStruct((y_size, cores, rows, x_size * out_cols), BF16),
        in_specs=[VMEM] * (1 + len(weights)),
        out_specs=VMEM,
        compiler_params=PARAMS,
        name="project",
    )(gated, *weights)
    parts = parts.reshape(y_size * cores, rows, x_size * out_cols)
    parts = exchange(parts, ("chan", "core")).reshape(y_size, cores, rows, x_size * out_cols)
    return pl.pallas_call(
        sum_kernel,
        out_shape=jax.ShapeDtypeStruct((rows, width), BF16),
        in_specs=[SMEM, VMEM],
        out_specs=VMEM,
        compiler_params=PARAMS,
        name="sum_parts",
    )(where, parts)


def solution(mesh):
    finer = Mesh(
        mesh.devices.reshape(8, 4, 2, mesh.shape["chan"]), ("z", "x", "core", "chan")
    )
    return jax.shard_map(
        body,
        mesh=finer,
        in_specs=(
            P(SEQ, "chan"),
            P(SEQ, "chan"),
            P(SEQ, "chan"),
            P(None, "chan"),
            P(None, "chan"),
            P("chan"),
            P("chan", SEQ),
        ),
        out_specs=P(SEQ, "chan"),
        check_vma=False,
    )
```

```python
import jax
import jax.numpy as jnp
from jax import lax
from jax.experimental import pallas as pl
from jax.experimental.pallas import tpu as pltpu
from jax.sharding import Mesh
from jax.sharding import PartitionSpec as P

F32 = jnp.float32
BF16 = jnp.bfloat16
SEQ = ("zh", "zl", "x", "core")
CHAN = ("yh", "yl")
LANES = 128
VMEM = pl.BlockSpec(memory_space=pltpu.VMEM)
SMEM = pl.BlockSpec(memory_space=pltpu.SMEM)
PARAMS = pltpu.CompilerParams(vmem_limit_bytes=48 * 1024 * 1024)


def tile_rows():
    return lax.broadcasted_iota(jnp.int32, (8, LANES), 0).astype(F32)


def own_rows_kernel(
    key_ref, value_ref, rate_ref, residue_ref, skip_ref, base_ref, state_ref, amp_ref, copy_ref
):
    rows, width = key_ref.shape
    modes = rate_ref.shape[0]
    tiles = rows // 8
    copies = state_ref.shape[0]

    def slab(index, carry):
        cols = pl.ds(pl.multiple_of(index * LANES, LANES), LANES)
        signal = key_ref[:, cols].astype(F32) * value_ref[:, cols].astype(F32)
        rate = rate_ref[:, cols]
        amp = residue_ref[:, cols] * jnp.sqrt(1.0 - jnp.exp(-2.0 * rate))
        amp_ref[:, cols] = amp
        copy_ref[:, cols] = rate
        steps = [jnp.exp(-8.0 * j * rate) for j in range(tiles)]
        scaled = [amp * step for step in steps]
        first = tile_rows()
        taps = [jnp.zeros((8, LANES), F32) for _ in range(tiles)]
        states = []
        for m in range(modes):
            ahead = jnp.exp(-rate[m : m + 1] * first)
            behind = jnp.exp(-rate[m : m + 1] * (7.0 - first))
            held = jnp.zeros((8, LANES), F32)
            for j in range(tiles):
                taps[j] = taps[j] + scaled[j][m : m + 1] * ahead
                held = held + steps[tiles - 1 - j][m : m + 1] * signal[8 * j : 8 * j + 8]
            states.append(jnp.sum(held * behind, axis=0, keepdims=True))
        state = jnp.concatenate(states, axis=0)
        for copy in range(copies):
            state_ref[copy, :, cols] = state
        row_ids = lax.broadcasted_iota(jnp.int32, (rows, LANES), 0)
        totals = [
            skip_ref[0:1, cols] * signal[8 * j : 8 * j + 8] for j in range(tiles)
        ]
        for lag in range(8):
            moved = signal
            if lag:
                moved = jnp.where(row_ids >= lag, pltpu.roll(signal, lag, 0), 0.0)
            for j in range(tiles):
                tap = taps[j][lag : lag + 1]
                for i in range(j, tiles):
                    totals[i] = totals[i] + tap * moved[8 * (i - j) : 8 * (i - j) + 8]
        for j in range(tiles):
            base_ref[8 * j : 8 * j + 8, cols] = totals[j]
        return carry

    lax.fori_loop(0, width // LANES, slab, 0)


def row_block_kernel(rows, where_ref, states_ref, rate_ref, before_ref, total_ref):
    own = where_ref[0]
    decay = jnp.exp(-float(rows) * rate_ref[...])
    running = jnp.zeros(rate_ref.shape, F32)
    before = jnp.zeros(rate_ref.shape, F32)
    for j in range(states_ref.shape[0]):
        before = jnp.where(own == j, running, before)
        running = decay * running + states_ref[j]
    before_ref[...] = before
    for copy in range(total_ref.shape[0]):
        total_ref[copy] = running


def gate_kernel(
    rows, where_ref, totals_ref, before_ref, rate_ref, amp_ref, base_ref, gate_ref, gated_ref
):
    own = where_ref[0].astype(F32)
    block = where_ref[1]
    blocks, modes, width = totals_ref.shape
    tiles = rows // 8

    def slab(index, carry):
        cols = pl.ds(pl.multiple_of(index * LANES, LANES), LANES)
        rate = rate_ref[:, cols]
        decay = jnp.exp(-float(rows * 8) * rate)
        running = jnp.zeros((modes, LANES), F32)
        entering = jnp.zeros((modes, LANES), F32)
        for z in range(blocks):
            entering = jnp.where(block == z, running, entering)
            running = decay * running + totals_ref[z, :, cols]
        state = before_ref[:, cols] + jnp.exp(-float(rows) * own * rate) * entering
        state = state * amp_ref[:, cols]
        scaled = [state * jnp.exp(-8.0 * j * rate) for j in range(tiles)]
        first = tile_rows() + 1.0
        totals = [base_ref[8 * j : 8 * j + 8, cols] for j in range(tiles)]
        for m in range(modes):
            ahead = jnp.exp(-rate[m : m + 1] * first)
            for j in range(tiles):
                totals[j] = totals[j] + scaled[j][m : m + 1] * ahead
        result = jnp.concatenate(totals, axis=0)
        gated_ref[:, cols] = (gate_ref[:, cols].astype(F32) * result).astype(BF16)
        return carry

    lax.fori_loop(0, width // LANES, slab, 0)


def project_kernel(gated_ref, weight_ref, out_ref):
    halves, cores, rows, depth = gated_ref.shape
    weight = weight_ref[...].reshape(-1, depth)
    for half in range(halves):
        gated = gated_ref[half].reshape(cores * rows, depth)
        part = lax.dot_general(
            gated, weight, (((1,), (1,)), ((), ())), preferred_element_type=F32
        ).astype(BF16)
        out_ref[half] = part.reshape(out_ref.shape[1:])


def sum_kernel(parts_ref, out_ref):
    total = parts_ref[0].astype(F32)
    for j in range(1, parts_ref.shape[0]):
        total = total + parts_ref[j].astype(F32)
    out_ref[...] = total.astype(BF16)


def interleave_kernel(unit, where_ref, pieces_ref, out_ref):
    own = where_ref[2]
    cores = pieces_ref.shape[0]
    pieces = [pieces_ref[core, own] for core in range(cores)]
    columns = []
    for j in range(pieces[0].shape[1] // unit):
        for piece in pieces:
            columns.append(piece[:, j * unit : (j + 1) * unit])
    out_ref[...] = jnp.concatenate(columns, axis=1)


def exchange(x, axes):
    return lax.all_to_all(x, axes, 0, 0, tiled=True)


def body(gate_input, key_input, value_input, decay_rate, residue, skip_gain, out_weight):
    rows, width = key_input.shape
    modes = decay_rate.shape[0]
    zh_size, zl_size, x_size, cores = (lax.axis_size(a) for a in SEQ)
    y_size = lax.axis_size(CHAN)
    z_size = zh_size * zl_size
    out_cols = out_weight.shape[1]
    where = jnp.stack(
        [lax.axis_index(("x", "core")), lax.axis_index(("zh", "zl")), lax.axis_index("core")]
    ).astype(jnp.int32)

    own_weight = jnp.broadcast_to(out_weight.T[None], (zh_size, out_cols, width))
    weight_z = exchange(own_weight, "zh")
    state_shape = jax.ShapeDtypeStruct((modes, width), F32)
    base, states, amplitude, rate = pl.pallas_call(
        own_rows_kernel,
        out_shape=(
            jax.ShapeDtypeStruct((rows, width), F32),
            jax.ShapeDtypeStruct((x_size * cores, modes, width), F32),
            state_shape,
            state_shape,
        ),
        in_specs=[VMEM] * 5,
        out_specs=(VMEM,) * 4,
        compiler_params=PARAMS,
        name="own_rows",
    )(key_input, value_input, decay_rate, residue, skip_gain[None, :])
    states, weight_z = lax.optimization_barrier((states, weight_z))
    weight = lax.all_gather(weight_z, "x")
    states = exchange(states, ("x", "core"))
    before, total = pl.pallas_call(
        lambda *refs: row_block_kernel(rows, *refs),
        out_shape=(
            jax.ShapeDtypeStruct((modes, width), F32),
            jax.ShapeDtypeStruct((z_size, modes, width), F32),
        ),
        in_specs=[SMEM, VMEM, VMEM],
        out_specs=(VMEM, VMEM),
        compiler_params=PARAMS,
        name="row_block",
    )(where, states, rate)
    totals = exchange(total, ("zh", "zl"))
    gated = pl.pallas_call(
        lambda *refs: gate_kernel(rows, *refs),
        out_shape=jax.ShapeDtypeStruct((rows, width), BF16),
        in_specs=[SMEM] + [VMEM] * 6,
        out_specs=VMEM,
        compiler_params=PARAMS,
        name="gate",
    )(where, totals, before, rate, amplitude, base, gate_input)
    gated = lax.all_gather(lax.all_gather(gated, "core"), "zl")
    piece = (cores, rows, x_size * out_cols)
    parts = pl.pallas_call(
        project_kernel,
        grid=(zh_size,),
        out_shape=jax.ShapeDtypeStruct((zh_size * zl_size,) + piece, BF16),
        in_specs=[
            pl.BlockSpec((zl_size, cores, rows, width), lambda i: (0, 0, 0, 0)),
            pl.BlockSpec((x_size, 1, out_cols, width), lambda i: (0, i, 0, 0)),
        ],
        out_specs=pl.BlockSpec((zl_size,) + piece, lambda i: (i, 0, 0, 0)),
        compiler_params=PARAMS,
        name="project",
    )(gated, weight)
    parts = exchange(parts, CHAN)
    summed = pl.pallas_call(
        sum_kernel,
        out_shape=jax.ShapeDtypeStruct(piece, BF16),
        in_specs=[VMEM],
        out_specs=VMEM,
        compiler_params=PARAMS,
        name="sum_parts",
    )(parts)
    swaps = [
        (zl * zl_size + yl, yl * zl_size + zl) for zl in range(zl_size) for yl in range(zl_size)
    ]
    summed = lax.ppermute(summed, ("zl", "yl"), swaps)
    summed = lax.all_gather(summed, "core")
    return pl.pallas_call(
        lambda *refs: interleave_kernel(out_cols, *refs),
        out_shape=jax.ShapeDtypeStruct((rows, width), BF16),
        in_specs=[SMEM, VMEM],
        out_specs=VMEM,
        compiler_params=PARAMS,
        name="interleave",
    )(where, summed)


def solution(mesh):
    finer = Mesh(mesh.devices.reshape(4, 2, 4, 2, 4, 2), SEQ + CHAN)
    return jax.shard_map(
        body,
        mesh=finer,
        in_specs=(
            P(SEQ, CHAN),
            P(SEQ, CHAN),
            P(SEQ, CHAN),
            P(None, CHAN),
            P(None, CHAN),
            P(CHAN),
            P(CHAN, SEQ),
        ),
        out_specs=P(SEQ, CHAN),
        check_vma=False,
    )
```

```python
import jax
import jax.numpy as jnp
from jax import lax
from jax.experimental import pallas as pl
from jax.experimental.pallas import tpu as pltpu
from jax.sharding import Mesh
from jax.sharding import PartitionSpec as P

F32 = jnp.float32
BF16 = jnp.bfloat16
SEQ = ("z", "xh", "xl", "core")
LANES = 128
VMEM = pl.BlockSpec(memory_space=pltpu.VMEM)
SMEM = pl.BlockSpec(memory_space=pltpu.SMEM)
PARAMS = pltpu.CompilerParams(vmem_limit_bytes=48 * 1024 * 1024)


def tile_rows():
    return lax.broadcasted_iota(jnp.int32, (8, LANES), 0).astype(F32)


def own_rows_kernel(
    key_ref, value_ref, rate_ref, residue_ref, skip_ref, base_ref, state_ref, amp_ref, copy_ref
):
    rows, width = key_ref.shape
    modes = rate_ref.shape[0]
    tiles = rows // 8

    def slab(index, carry):
        cols = pl.ds(pl.multiple_of(index * LANES, LANES), LANES)
        signal = key_ref[:, cols].astype(F32) * value_ref[:, cols].astype(F32)
        rate = rate_ref[:, cols]
        amp = residue_ref[:, cols] * jnp.sqrt(1.0 - jnp.exp(-2.0 * rate))
        amp_ref[:, cols] = amp
        copy_ref[:, cols] = rate
        steps = [jnp.exp(-8.0 * j * rate) for j in range(tiles)]
        scaled = [amp * step for step in steps]
        first = tile_rows()
        taps = [jnp.zeros((8, LANES), F32) for _ in range(tiles)]
        states = []
        for m in range(modes):
            ahead = jnp.exp(-rate[m : m + 1] * first)
            behind = jnp.exp(-rate[m : m + 1] * (7.0 - first))
            held = jnp.zeros((8, LANES), F32)
            for j in range(tiles):
                taps[j] = taps[j] + scaled[j][m : m + 1] * ahead
                held = held + steps[tiles - 1 - j][m : m + 1] * signal[8 * j : 8 * j + 8]
            states.append(jnp.sum(held * behind, axis=0, keepdims=True))
        state_ref[:, cols] = jnp.concatenate(states, axis=0)
        row_ids = lax.broadcasted_iota(jnp.int32, (rows, LANES), 0)
        totals = [
            skip_ref[0:1, cols] * signal[8 * j : 8 * j + 8] for j in range(tiles)
        ]
        for lag in range(8):
            moved = signal
            if lag:
                moved = jnp.where(row_ids >= lag, pltpu.roll(signal, lag, 0), 0.0)
            for j in range(tiles):
                tap = taps[j][lag : lag + 1]
                for i in range(j, tiles):
                    totals[i] = totals[i] + tap * moved[8 * (i - j) : 8 * (i - j) + 8]
        for j in range(tiles):
            base_ref[8 * j : 8 * j + 8, cols] = totals[j]
        return carry

    lax.fori_loop(0, width // LANES, slab, 0)


def row_block_kernel(rows, where_ref, states_ref, rate_ref, before_ref, total_ref):
    own = where_ref[0]
    decay = jnp.exp(-float(rows) * rate_ref[...])
    running = jnp.zeros(rate_ref.shape, F32)
    before = jnp.zeros(rate_ref.shape, F32)
    for j in range(states_ref.shape[0]):
        before = jnp.where(own == j, running, before)
        running = decay * running + states_ref[j]
    before_ref[...] = before
    for copy in range(total_ref.shape[0]):
        total_ref[copy] = running


def gate_kernel(
    rows, where_ref, totals_ref, before_ref, rate_ref, amp_ref, base_ref, gate_ref, gated_ref
):
    own = where_ref[0].astype(F32)
    block = where_ref[1]
    blocks, modes, width = totals_ref.shape
    tiles = rows // 8

    def slab(index, carry):
        cols = pl.ds(pl.multiple_of(index * LANES, LANES), LANES)
        rate = rate_ref[:, cols]
        decay = jnp.exp(-float(rows * 8) * rate)
        running = jnp.zeros((modes, LANES), F32)
        entering = jnp.zeros((modes, LANES), F32)
        for z in range(blocks):
            entering = jnp.where(block == z, running, entering)
            running = decay * running + totals_ref[z, :, cols]
        state = before_ref[:, cols] + jnp.exp(-float(rows) * own * rate) * entering
        state = state * amp_ref[:, cols]
        scaled = [state * jnp.exp(-8.0 * j * rate) for j in range(tiles)]
        first = tile_rows() + 1.0
        totals = [base_ref[8 * j : 8 * j + 8, cols] for j in range(tiles)]
        for m in range(modes):
            ahead = jnp.exp(-rate[m : m + 1] * first)
            for j in range(tiles):
                totals[j] = totals[j] + scaled[j][m : m + 1] * ahead
        result = jnp.concatenate(totals, axis=0)
        gated_ref[:, cols] = (gate_ref[:, cols].astype(F32) * result).astype(BF16)
        return carry

    lax.fori_loop(0, width // LANES, slab, 0)


def project_kernel(gated_ref, near_ref, far_ref, out_ref):
    shared, rows, depth = gated_ref.shape
    gated = gated_ref[...].reshape(shared * rows, depth)
    for j in range(out_ref.shape[0]):
        weight = jnp.concatenate([near_ref[j], far_ref[j]], axis=0)
        part = lax.dot_general(
            gated, weight, (((1,), (1,)), ((), ())), preferred_element_type=F32
        ).astype(BF16)
        out_ref[j] = part.reshape(out_ref.shape[1:])


def sum_kernel(where_ref, parts_ref, out_ref):
    groups, low, cores, rows, width = parts_ref.shape
    own_high = where_ref[2]
    unit = width // 2
    for x_low in range(low):
        totals = []
        for core in range(cores):
            total = parts_ref[0, x_low, core].astype(F32)
            for j in range(1, groups):
                total = total + parts_ref[j, x_low, core].astype(F32)
            totals.append(total)
        for far in range(2):
            high = own_high if far == 0 else 1 - own_high
            place = pl.multiple_of((high * low + x_low) * (cores * unit), cores * unit)
            pieces = [total[:, far * unit : (far + 1) * unit] for total in totals]
            columns = jnp.concatenate(pieces, axis=1)
            out_ref[:, pl.ds(place, cores * unit)] = columns.astype(BF16)


def exchange(x, axes):
    return lax.all_to_all(x, axes, 0, 0, tiled=True)


def body(gate_input, key_input, value_input, decay_rate, residue, skip_gain, out_weight):
    rows, width = key_input.shape
    modes = decay_rate.shape[0]
    z_size, high_size, low_size, cores = (lax.axis_size(a) for a in SEQ)
    y_size = lax.axis_size("chan")
    out_cols = out_weight.shape[1]
    where = jnp.stack(
        [lax.axis_index(("xh", "xl", "core")), lax.axis_index("z"), lax.axis_index("xh")]
    ).astype(jnp.int32)

    own_weight = jnp.broadcast_to(out_weight.T[None], (z_size, out_cols, width))
    near = exchange(own_weight, "z")
    state_shape = jax.ShapeDtypeStruct((modes, width), F32)
    base, state, amplitude, rate = pl.pallas_call(
        own_rows_kernel,
        out_shape=(jax.ShapeDtypeStruct((rows, width), F32),) + (state_shape,) * 3,
        in_specs=[VMEM] * 5,
        out_specs=(VMEM,) * 4,
        compiler_params=PARAMS,
        name="own_rows",
    )(key_input, value_input, decay_rate, residue, skip_gain[None, :])
    states = lax.all_gather(lax.all_gather(state, "core"), ("xh", "xl"))
    states = states.reshape(-1, modes, width)
    states, near = lax.optimization_barrier((states, near))
    far = lax.ppermute(near, "xh", [(0, 1), (1, 0)])
    before, total = pl.pallas_call(
        lambda *refs: row_block_kernel(rows, *refs),
        out_shape=(
            jax.ShapeDtypeStruct((modes, width), F32),
            jax.ShapeDtypeStruct((z_size, modes, width), F32),
        ),
        in_specs=[SMEM, VMEM, VMEM],
        out_specs=(VMEM, VMEM),
        compiler_params=PARAMS,
        name="row_block",
    )(where, states, rate)
    totals = exchange(total, "z")
    gated = pl.pallas_call(
        lambda *refs: gate_kernel(rows, *refs),
        out_shape=jax.ShapeDtypeStruct((rows, width), BF16),
        in_specs=[SMEM] + [VMEM] * 6,
        out_specs=VMEM,
        compiler_params=PARAMS,
        name="gate",
    )(where, totals, before, rate, amplitude, base, gate_input)
    gated = lax.all_gather(lax.all_gather(gated, "core"), "xl")
    shared = low_size * cores
    piece = (rows, high_size * out_cols)
    parts = pl.pallas_call(
        project_kernel,
        out_shape=jax.ShapeDtypeStruct((y_size, shared) + piece, BF16),
        in_specs=[VMEM] * 3,
        out_specs=VMEM,
        compiler_params=PARAMS,
        name="project",
    )(gated.reshape(shared, rows, width), near, far)
    parts = exchange(parts.reshape((y_size * shared,) + piece), ("chan", "xl", "core"))
    return pl.pallas_call(
        sum_kernel,
        out_shape=jax.ShapeDtypeStruct((rows, width), BF16),
        in_specs=[SMEM, VMEM],
        out_specs=VMEM,
        compiler_params=PARAMS,
        name="sum_parts",
    )(where, parts.reshape((y_size, low_size, cores) + piece))


def solution(mesh):
    finer = Mesh(mesh.devices.reshape(8, 2, 2, 2, 8), SEQ + ("chan",))
    return jax.shard_map(
        body,
        mesh=finer,
        in_specs=(
            P(SEQ, "chan"),
            P(SEQ, "chan"),
            P(SEQ, "chan"),
            P(None, "chan"),
            P(None, "chan"),
            P("chan"),
            P("chan", SEQ),
        ),
        out_specs=P(SEQ, "chan"),
        check_vma=False,
    )
```

```python
import jax
import jax.numpy as jnp
from jax import lax
from jax.experimental import pallas as pl
from jax.experimental.pallas import tpu as pltpu
from jax.sharding import Mesh
from jax.sharding import PartitionSpec as P

F32 = jnp.float32
BF16 = jnp.bfloat16
SEQ = ("z", "xh", "xl", "core")
LANES = 128
VMEM = pl.BlockSpec(memory_space=pltpu.VMEM)
SMEM = pl.BlockSpec(memory_space=pltpu.SMEM)
PARAMS = pltpu.CompilerParams(vmem_limit_bytes=48 * 1024 * 1024)


def tile_rows():
    return lax.broadcasted_iota(jnp.int32, (8, LANES), 0).astype(F32)


def chunk_kernel(
    where_ref, signals_ref, rate_ref, residue_ref, skip_ref,
    base_ref, before_ref, send_ref, amp_ref, copy_ref, signal_ref, state_ref,
):
    blocks, rows, width = base_ref.shape
    modes = rate_ref.shape[0]
    tiles = rows // 8
    cores = signals_ref.shape[0]
    first_col = where_ref[1] * width

    def slab(index, carry):
        cols = pl.ds(pl.multiple_of(index * LANES, LANES), LANES)
        source = pl.ds(pl.multiple_of(first_col + index * LANES, LANES), LANES)
        for i in range(blocks):
            signal_ref[i] = signals_ref[i % cores, i // cores, :, source]
        rate = rate_ref[:, source]
        amp = residue_ref[:, source] * jnp.sqrt(1.0 - jnp.exp(-2.0 * rate))
        amp_ref[:, cols] = amp
        copy_ref[:, cols] = rate
        steps = [jnp.exp(-8.0 * j * rate) for j in range(tiles)]
        scaled = [amp * step for step in steps]
        first = tile_rows()
        taps = [jnp.zeros((8, LANES), F32) for _ in range(tiles)]
        for m in range(modes):
            ahead = jnp.exp(-rate[m : m + 1] * first)
            behind = jnp.exp(-rate[m : m + 1] * (7.0 - first))
            held = [jnp.zeros((8, LANES), F32) for _ in range(blocks)]
            for j in range(tiles):
                taps[j] = taps[j] + scaled[j][m : m + 1] * ahead
                step = steps[tiles - 1 - j][m : m + 1]
                for i in range(blocks):
                    held[i] = held[i] + step * signal_ref[i, 8 * j : 8 * j + 8]
            for i in range(blocks):
                state_ref[i, m : m + 1] = jnp.sum(held[i] * behind, axis=0, keepdims=True)
        decay = jnp.exp(-float(rows) * rate)
        running = jnp.zeros((modes, LANES), F32)
        for i in range(blocks):
            before_ref[i, :, cols] = running
            running = decay * running + state_ref[i]
        for copy in range(send_ref.shape[0]):
            send_ref[copy, :, cols] = running
        row_ids = lax.broadcasted_iota(jnp.int32, (rows, LANES), 0)
        skip = skip_ref[0:1, source]

        def block(i, inner):
            signal = signal_ref[i]
            totals = [skip * signal[8 * j : 8 * j + 8] for j in range(tiles)]
            for lag in range(8):
                moved = signal
                if lag:
                    moved = jnp.where(row_ids >= lag, pltpu.roll(signal, lag, 0), 0.0)
                for j in range(tiles):
                    tap = taps[j][lag : lag + 1]
                    for k in range(j, tiles):
                        totals[k] = totals[k] + tap * moved[8 * (k - j) : 8 * (k - j) + 8]
            for j in range(tiles):
                base_ref[i, 8 * j : 8 * j + 8, cols] = totals[j]
            return inner

        return lax.fori_loop(0, blocks, block, carry)

    lax.fori_loop(0, width // LANES, slab, 0)


def gate_kernel(
    where_ref, chunks_ref, before_ref, rate_ref, amp_ref, base_ref, gate_ref, gated_ref
):
    blocks, rows, width = base_ref.shape
    modes = rate_ref.shape[0]
    tiles = rows // 8
    cores = gate_ref.shape[0]
    own = where_ref[0]
    first_col = where_ref[1] * width

    def slab(index, carry):
        cols = pl.ds(pl.multiple_of(index * LANES, LANES), LANES)
        source = pl.ds(pl.multiple_of(first_col + index * LANES, LANES), LANES)
        rate = rate_ref[:, cols]
        amp = amp_ref[:, cols]
        decay = jnp.exp(-float(rows * blocks) * rate)
        running = jnp.zeros((modes, LANES), F32)
        entering = jnp.zeros((modes, LANES), F32)
        for chunk in range(chunks_ref.shape[0]):
            entering = jnp.where(own == chunk, running, entering)
            running = decay * running + chunks_ref[chunk, :, cols]
        steps = [jnp.exp(-8.0 * j * rate) for j in range(tiles)]
        first = tile_rows() + 1.0
        aheads = [jnp.exp(-rate[m : m + 1] * first) for m in range(modes)]
        state = entering
        for i in range(blocks):
            full = (before_ref[i, :, cols] + state) * amp
            if i < blocks - 1:
                state = state * jnp.exp(-float(rows) * rate)
            for j in range(tiles):
                part = base_ref[i, 8 * j : 8 * j + 8, cols]
                scaled = full * steps[j]
                for m in range(modes):
                    part = part + scaled[m : m + 1] * aheads[m]
                gate = gate_ref[i % cores, i // cores, 8 * j : 8 * j + 8, source].astype(F32)
                gated_ref[i, 8 * j : 8 * j + 8, cols] = (gate * part).astype(BF16)
        return carry

    lax.fori_loop(0, width // LANES, slab, 0)


def project_kernel(gated_ref, near_ref, far_ref, out_ref):
    cores, shared, rows, half = gated_ref.shape
    gated = [gated_ref[core].reshape(shared * rows, half) for core in range(cores)]
    for j in range(out_ref.shape[0]):
        total = 0.0
        for core in range(cores):
            depth = slice(core * half, (core + 1) * half)
            weight = jnp.concatenate([near_ref[j, :, depth], far_ref[j, :, depth]], axis=0)
            total = total + lax.dot_general(
                gated[core], weight, (((1,), (1,)), ((), ())), preferred_element_type=F32
            )
        out_ref[j] = total.astype(BF16).reshape(out_ref.shape[1:])


def sum_kernel(where_ref, parts_ref, out_ref):
    groups, low, cores, rows, width = parts_ref.shape
    own_high = where_ref[2]
    unit = width // 2
    for x_low in range(low):
        totals = []
        for core in range(cores):
            total = parts_ref[0, x_low, core].astype(F32)
            for j in range(1, groups):
                total = total + parts_ref[j, x_low, core].astype(F32)
            totals.append(total)
        for far in range(2):
            high = own_high if far == 0 else 1 - own_high
            place = pl.multiple_of((high * low + x_low) * (cores * unit), cores * unit)
            pieces = [total[:, far * unit : (far + 1) * unit] for total in totals]
            columns = jnp.concatenate(pieces, axis=1)
            out_ref[:, pl.ds(place, cores * unit)] = columns.astype(BF16)


def exchange(x, axes):
    return lax.all_to_all(x, axes, 0, 0, tiled=True)


def body(gate_input, key_input, value_input, decay_rate, residue, skip_gain, out_weight):
    rows, width = key_input.shape
    modes = decay_rate.shape[0]
    z_size, high_size, low_size, cores = (lax.axis_size(a) for a in SEQ)
    y_size = lax.axis_size("chan")
    out_cols = out_weight.shape[1]
    chunks = z_size * high_size
    blocks = low_size * cores
    half = width // cores
    where = jnp.stack(
        [lax.axis_index(("z", "xh")), lax.axis_index("core"), lax.axis_index("xh")]
    ).astype(jnp.int32)

    own_weight = jnp.broadcast_to(out_weight.T[None], (z_size, out_cols, width))
    near = exchange(own_weight, "z")
    signal = key_input.astype(F32) * value_input.astype(F32)
    signals = lax.all_gather(lax.all_gather(signal, "xl"), "core")
    gate = lax.all_gather(lax.all_gather(gate_input, "xl"), "core")
    base, before, state, amplitude, rate = pl.pallas_call(
        chunk_kernel,
        out_shape=(
            jax.ShapeDtypeStruct((blocks, rows, half), F32),
            jax.ShapeDtypeStruct((blocks, modes, half), F32),
            jax.ShapeDtypeStruct((chunks, modes, half), F32),
            jax.ShapeDtypeStruct((modes, half), F32),
            jax.ShapeDtypeStruct((modes, half), F32),
        ),
        in_specs=[SMEM] + [VMEM] * 4,
        out_specs=(VMEM,) * 5,
        scratch_shapes=[
            pltpu.VMEM((blocks, rows, LANES), F32),
            pltpu.VMEM((blocks, modes, LANES), F32),
        ],
        compiler_params=PARAMS,
        name="chunk",
    )(where, signals, decay_rate, residue, skip_gain[None, :])
    state, near = lax.optimization_barrier((state, near))
    far = lax.ppermute(near, "xh", [(0, 1), (1, 0)])
    states = exchange(state, ("z", "xh"))
    gated = pl.pallas_call(
        gate_kernel,
        out_shape=jax.ShapeDtypeStruct((blocks, rows, half), BF16),
        in_specs=[SMEM] + [VMEM] * 6,
        out_specs=VMEM,
        compiler_params=PARAMS,
        name="gate",
    )(where, states, before, rate, amplitude, base, gate)
    gated = lax.all_gather(gated, "core")
    piece = (rows, high_size * out_cols)
    parts = pl.pallas_call(
        project_kernel,
        out_shape=jax.ShapeDtypeStruct((y_size, blocks) + piece, BF16),
        in_specs=[VMEM] * 3,
        out_specs=VMEM,
        compiler_params=PARAMS,
        name="project",
    )(gated, near, far)
    parts = exchange(parts.reshape((y_size * blocks,) + piece), ("chan", "xl", "core"))
    return pl.pallas_call(
        sum_kernel,
        out_shape=jax.ShapeDtypeStruct((rows, width), BF16),
        in_specs=[SMEM, VMEM],
        out_specs=VMEM,
        compiler_params=PARAMS,
        name="sum_parts",
    )(where, parts.reshape((y_size, low_size, cores) + piece))


def solution(mesh):
    finer = Mesh(mesh.devices.reshape(8, 2, 2, 2, 8), SEQ + ("chan",))
    return jax.shard_map(
        body,
        mesh=finer,
        in_specs=(
            P(SEQ, "chan"),
            P(SEQ, "chan"),
            P(SEQ, "chan"),
            P(None, "chan"),
            P(None, "chan"),
            P("chan"),
            P("chan", SEQ),
        ),
        out_specs=P(SEQ, "chan"),
        check_vma=False,
    )
```

```python
import jax
import jax.numpy as jnp
from jax import lax
from jax.experimental import pallas as pl
from jax.experimental.pallas import tpu as pltpu
from jax.sharding import Mesh
from jax.sharding import PartitionSpec as P

F32 = jnp.float32
BF16 = jnp.bfloat16
SEQ = ("z", "xh", "xl", "core")
LANES = 128
VMEM = pl.BlockSpec(memory_space=pltpu.VMEM)
SMEM = pl.BlockSpec(memory_space=pltpu.SMEM)
PARAMS = pltpu.CompilerParams(vmem_limit_bytes=48 * 1024 * 1024)


def tile_rows():
    return lax.broadcasted_iota(jnp.int32, (8, LANES), 0).astype(F32)


def chunk_kernel(
    where_ref, inputs_ref, rate_ref, residue_ref, skip_ref,
    base_ref, before_ref, send_ref, amp_ref, copy_ref, signal_ref, state_ref,
):
    blocks, rows, width = base_ref.shape
    modes = rate_ref.shape[0]
    tiles = rows // 8
    cores = inputs_ref.shape[0]
    first_col = where_ref[1] * width

    def slab(index, carry):
        cols = pl.ds(pl.multiple_of(index * LANES, LANES), LANES)
        source = pl.ds(pl.multiple_of(first_col + index * LANES, LANES), LANES)
        for i in range(blocks):
            key = inputs_ref[i % cores, i // cores, 0, :, source].astype(F32)
            signal_ref[i] = key * inputs_ref[i % cores, i // cores, 1, :, source].astype(F32)
        rate = rate_ref[:, source]
        amp = residue_ref[:, source] * jnp.sqrt(1.0 - jnp.exp(-2.0 * rate))
        amp_ref[:, cols] = amp
        copy_ref[:, cols] = rate
        steps = [jnp.exp(-8.0 * j * rate) for j in range(tiles)]
        scaled = [amp * step for step in steps]
        first = tile_rows()
        taps = [jnp.zeros((8, LANES), F32) for _ in range(tiles)]
        for m in range(modes):
            ahead = jnp.exp(-rate[m : m + 1] * first)
            behind = jnp.exp(-rate[m : m + 1] * (7.0 - first))
            held = [jnp.zeros((8, LANES), F32) for _ in range(blocks)]
            for j in range(tiles):
                taps[j] = taps[j] + scaled[j][m : m + 1] * ahead
                step = steps[tiles - 1 - j][m : m + 1]
                for i in range(blocks):
                    held[i] = held[i] + step * signal_ref[i, 8 * j : 8 * j + 8]
            for i in range(blocks):
                state_ref[i, m : m + 1] = jnp.sum(held[i] * behind, axis=0, keepdims=True)
        decay = jnp.exp(-float(rows) * rate)
        running = jnp.zeros((modes, LANES), F32)
        for i in range(blocks):
            before_ref[i, :, cols] = running
            running = decay * running + state_ref[i]
        for copy in range(send_ref.shape[0]):
            send_ref[copy, :, cols] = running
        row_ids = lax.broadcasted_iota(jnp.int32, (rows, LANES), 0)
        skip = skip_ref[0:1, source]

        def block(i, inner):
            signal = signal_ref[i]
            totals = [skip * signal[8 * j : 8 * j + 8] for j in range(tiles)]
            for lag in range(8):
                moved = signal
                if lag:
                    moved = jnp.where(row_ids >= lag, pltpu.roll(signal, lag, 0), 0.0)
                for j in range(tiles):
                    tap = taps[j][lag : lag + 1]
                    for k in range(j, tiles):
                        totals[k] = totals[k] + tap * moved[8 * (k - j) : 8 * (k - j) + 8]
            for j in range(tiles):
                base_ref[i, 8 * j : 8 * j + 8, cols] = totals[j]
            return inner

        return lax.fori_loop(0, blocks, block, carry)

    lax.fori_loop(0, width // LANES, slab, 0)


def gate_kernel(
    where_ref, chunks_ref, before_ref, rate_ref, amp_ref, base_ref, inputs_ref, gated_ref
):
    blocks, rows, width = base_ref.shape
    modes = rate_ref.shape[0]
    tiles = rows // 8
    cores = inputs_ref.shape[0]
    own = where_ref[0]
    first_col = where_ref[1] * width

    def slab(index, carry):
        cols = pl.ds(pl.multiple_of(index * LANES, LANES), LANES)
        source = pl.ds(pl.multiple_of(first_col + index * LANES, LANES), LANES)
        rate = rate_ref[:, cols]
        amp = amp_ref[:, cols]
        decay = jnp.exp(-float(rows * blocks) * rate)
        running = jnp.zeros((modes, LANES), F32)
        entering = jnp.zeros((modes, LANES), F32)
        for chunk in range(chunks_ref.shape[0]):
            entering = jnp.where(own == chunk, running, entering)
            running = decay * running + chunks_ref[chunk, :, cols]
        steps = [jnp.exp(-8.0 * j * rate) for j in range(tiles)]
        first = tile_rows() + 1.0
        aheads = [jnp.exp(-rate[m : m + 1] * first) for m in range(modes)]
        state = entering
        for i in range(blocks):
            full = (before_ref[i, :, cols] + state) * amp
            if i < blocks - 1:
                state = state * jnp.exp(-float(rows) * rate)
            parts = []
            for j in range(tiles):
                part = base_ref[i, 8 * j : 8 * j + 8, cols]
                scaled = full * steps[j]
                for m in range(modes):
                    part = part + scaled[m : m + 1] * aheads[m]
                parts.append(part)
            gate = inputs_ref[i % cores, i // cores, 2, :, source].astype(F32)
            gated_ref[i, :, cols] = (gate * jnp.concatenate(parts, axis=0)).astype(BF16)
        return carry

    lax.fori_loop(0, width // LANES, slab, 0)


def project_kernel(gated_ref, near_ref, far_ref, out_ref):
    cores, shared, rows, half = gated_ref.shape
    gated = [gated_ref[core].reshape(shared * rows, half) for core in range(cores)]
    for j in range(out_ref.shape[0]):
        total = 0.0
        for core in range(cores):
            depth = slice(core * half, (core + 1) * half)
            weight = jnp.concatenate([near_ref[j, :, depth], far_ref[j, :, depth]], axis=0)
            total = total + lax.dot_general(
                gated[core], weight, (((1,), (1,)), ((), ())), preferred_element_type=F32
            )
        out_ref[j] = total.astype(BF16).reshape(out_ref.shape[1:])


def sum_kernel(where_ref, parts_ref, out_ref):
    groups, low, cores, rows, width = parts_ref.shape
    own_high = where_ref[2]
    unit = width // 2
    for x_low in range(low):
        totals = []
        for core in range(cores):
            total = parts_ref[0, x_low, core].astype(F32)
            for j in range(1, groups):
                total = total + parts_ref[j, x_low, core].astype(F32)
            totals.append(total)
        for far in range(2):
            high = own_high if far == 0 else 1 - own_high
            place = pl.multiple_of((high * low + x_low) * (cores * unit), cores * unit)
            pieces = [total[:, far * unit : (far + 1) * unit] for total in totals]
            columns = jnp.concatenate(pieces, axis=1)
            out_ref[:, pl.ds(place, cores * unit)] = columns.astype(BF16)


def exchange(x, axes):
    return lax.all_to_all(x, axes, 0, 0, tiled=True)


def body(gate_input, key_input, value_input, decay_rate, residue, skip_gain, out_weight):
    rows, width = key_input.shape
    modes = decay_rate.shape[0]
    z_size, high_size, low_size, cores = (lax.axis_size(a) for a in SEQ)
    y_size = lax.axis_size("chan")
    out_cols = out_weight.shape[1]
    chunks = z_size * high_size
    blocks = low_size * cores
    half = width // cores
    where = jnp.stack(
        [lax.axis_index(("z", "xh")), lax.axis_index("core"), lax.axis_index("xh")]
    ).astype(jnp.int32)

    own_weight = jnp.broadcast_to(out_weight.T[None], (z_size, out_cols, width))
    near = exchange(own_weight, "z")
    inputs = jnp.stack([key_input, value_input, gate_input])
    inputs = lax.all_gather(lax.all_gather(inputs, "xl"), "core")
    base, before, state, amplitude, rate = pl.pallas_call(
        chunk_kernel,
        out_shape=(
            jax.ShapeDtypeStruct((blocks, rows, half), F32),
            jax.ShapeDtypeStruct((blocks, modes, half), F32),
            jax.ShapeDtypeStruct((chunks, modes, half), F32),
            jax.ShapeDtypeStruct((modes, half), F32),
            jax.ShapeDtypeStruct((modes, half), F32),
        ),
        in_specs=[SMEM] + [VMEM] * 4,
        out_specs=(VMEM,) * 5,
        scratch_shapes=[
            pltpu.VMEM((blocks, rows, LANES), F32),
            pltpu.VMEM((blocks, modes, LANES), F32),
        ],
        compiler_params=PARAMS,
        name="chunk",
    )(where, inputs, decay_rate, residue, skip_gain[None, :])
    state, near = lax.optimization_barrier((state, near))
    far = lax.ppermute(near, "xh", [(0, 1), (1, 0)])
    states = exchange(state, ("z", "xh"))
    gated = pl.pallas_call(
        gate_kernel,
        out_shape=jax.ShapeDtypeStruct((blocks, rows, half), BF16),
        in_specs=[SMEM] + [VMEM] * 6,
        out_specs=VMEM,
        compiler_params=PARAMS,
        name="gate",
    )(where, states, before, rate, amplitude, base, inputs)
    gated = lax.all_gather(gated, "core")
    piece = (rows, high_size * out_cols)
    parts = pl.pallas_call(
        project_kernel,
        out_shape=jax.ShapeDtypeStruct((y_size, blocks) + piece, BF16),
        in_specs=[VMEM] * 3,
        out_specs=VMEM,
        compiler_params=PARAMS,
        name="project",
    )(gated, near, far)
    parts = exchange(parts.reshape((y_size * blocks,) + piece), ("chan", "xl", "core"))
    return pl.pallas_call(
        sum_kernel,
        out_shape=jax.ShapeDtypeStruct((rows, width), BF16),
        in_specs=[SMEM, VMEM],
        out_specs=VMEM,
        compiler_params=PARAMS,
        name="sum_parts",
    )(where, parts.reshape((y_size, low_size, cores) + piece))


def solution(mesh):
    finer = Mesh(mesh.devices.reshape(8, 2, 2, 2, 8), SEQ + ("chan",))
    return jax.shard_map(
        body,
        mesh=finer,
        in_specs=(
            P(SEQ, "chan"),
            P(SEQ, "chan"),
            P(SEQ, "chan"),
            P(None, "chan"),
            P(None, "chan"),
            P("chan"),
            P("chan", SEQ),
        ),
        out_specs=P(SEQ, "chan"),
        check_vma=False,
    )
```

```python
import jax
import jax.numpy as jnp
from jax import lax
from jax.experimental import pallas as pl
from jax.experimental.pallas import tpu as pltpu
from jax.sharding import Mesh
from jax.sharding import PartitionSpec as P

F32 = jnp.float32
BF16 = jnp.bfloat16
SEQ = ("z", "xh", "xl", "core")
LANES = 128
VMEM = pl.BlockSpec(memory_space=pltpu.VMEM)
SMEM = pl.BlockSpec(memory_space=pltpu.SMEM)
PARAMS = pltpu.CompilerParams(vmem_limit_bytes=48 * 1024 * 1024)


def tile_rows():
    return lax.broadcasted_iota(jnp.int32, (8, LANES), 0).astype(F32)


def chunk_kernel(
    where_ref, inputs_ref, rate_ref, residue_ref, skip_ref,
    base_ref, before_ref, send_ref, amp_ref, copy_ref, signal_ref, state_ref,
):
    blocks, rows, width = base_ref.shape
    modes = rate_ref.shape[0]
    tiles = rows // 8
    cores = inputs_ref.shape[0]
    first_col = where_ref[1] * width

    def slab(index, carry):
        cols = pl.ds(pl.multiple_of(index * LANES, LANES), LANES)
        source = pl.ds(pl.multiple_of(first_col + index * LANES, LANES), LANES)
        for i in range(blocks):
            key = inputs_ref[i % cores, i // cores, 0, :, source].astype(F32)
            signal_ref[i] = key * inputs_ref[i % cores, i // cores, 1, :, source].astype(F32)
        rate = rate_ref[:, source]
        amp = residue_ref[:, source] * jnp.sqrt(1.0 - jnp.exp(-2.0 * rate))
        amp_ref[:, cols] = amp
        copy_ref[:, cols] = rate
        steps = [jnp.exp(-8.0 * j * rate) for j in range(tiles)]
        scaled = [amp * step for step in steps]
        first = tile_rows()
        taps = [jnp.zeros((8, LANES), F32) for _ in range(tiles)]
        for m in range(modes):
            ahead = jnp.exp(-rate[m : m + 1] * first)
            behind = jnp.exp(-rate[m : m + 1] * (7.0 - first))
            held = [jnp.zeros((8, LANES), F32) for _ in range(blocks)]
            for j in range(tiles):
                taps[j] = taps[j] + scaled[j][m : m + 1] * ahead
                step = steps[tiles - 1 - j][m : m + 1]
                for i in range(blocks):
                    held[i] = held[i] + step * signal_ref[i, 8 * j : 8 * j + 8]
            for i in range(blocks):
                state_ref[i, m : m + 1] = jnp.sum(held[i] * behind, axis=0, keepdims=True)
        decay = jnp.exp(-float(rows) * rate)
        running = jnp.zeros((modes, LANES), F32)
        for i in range(blocks):
            before_ref[i, :, cols] = running
            running = decay * running + state_ref[i]
        for copy in range(send_ref.shape[0]):
            send_ref[copy, :, cols] = running
        row_ids = lax.broadcasted_iota(jnp.int32, (rows, LANES), 0)
        skip = skip_ref[0:1, source]

        def block(i, inner):
            signal = signal_ref[i]
            totals = [skip * signal[8 * j : 8 * j + 8] for j in range(tiles)]
            for lag in range(8):
                moved = signal
                if lag:
                    moved = jnp.where(row_ids >= lag, pltpu.roll(signal, lag, 0), 0.0)
                for j in range(tiles):
                    tap = taps[j][lag : lag + 1]
                    for k in range(j, tiles):
                        totals[k] = totals[k] + tap * moved[8 * (k - j) : 8 * (k - j) + 8]
            for j in range(tiles):
                base_ref[i, 8 * j : 8 * j + 8, cols] = totals[j]
            return inner

        return lax.fori_loop(0, blocks, block, carry)

    lax.fori_loop(0, width // LANES, slab, 0)


def gate_kernel(
    where_ref, chunks_ref, before_ref, rate_ref, amp_ref, base_ref, inputs_ref, gated_ref
):
    blocks, rows, width = base_ref.shape
    modes = rate_ref.shape[0]
    tiles = rows // 8
    cores = inputs_ref.shape[0]
    own = where_ref[0]
    first_col = where_ref[1] * width

    def slab(index, carry):
        cols = pl.ds(pl.multiple_of(index * LANES, LANES), LANES)
        source = pl.ds(pl.multiple_of(first_col + index * LANES, LANES), LANES)
        rate = rate_ref[:, cols]
        amp = amp_ref[:, cols]
        decay = jnp.exp(-float(rows * blocks) * rate)
        running = jnp.zeros((modes, LANES), F32)
        entering = jnp.zeros((modes, LANES), F32)
        for chunk in range(chunks_ref.shape[0]):
            entering = jnp.where(own == chunk, running, entering)
            running = decay * running + chunks_ref[chunk, :, cols]
        steps = [jnp.exp(-8.0 * j * rate) for j in range(tiles)]
        first = tile_rows() + 1.0
        aheads = [jnp.exp(-rate[m : m + 1] * first) for m in range(modes)]
        state = entering
        for i in range(blocks):
            full = (before_ref[i, :, cols] + state) * amp
            if i < blocks - 1:
                state = state * jnp.exp(-float(rows) * rate)
            parts = []
            for j in range(tiles):
                part = base_ref[i, 8 * j : 8 * j + 8, cols]
                scaled = full * steps[j]
                for m in range(modes):
                    part = part + scaled[m : m + 1] * aheads[m]
                parts.append(part)
            gate = inputs_ref[i % cores, i // cores, 2, :, source].astype(F32)
            gated_ref[i, :, cols] = (gate * jnp.concatenate(parts, axis=0)).astype(BF16)
        return carry

    lax.fori_loop(0, width // LANES, slab, 0)


def project_kernel(gated_ref, near_ref, far_ref, out_ref):
    cores, shared, rows, half = gated_ref.shape
    gated = [gated_ref[core].reshape(shared * rows, half) for core in range(cores)]
    for j in range(out_ref.shape[0]):
        total = 0.0
        for core in range(cores):
            depth = slice(core * half, (core + 1) * half)
            weight = jnp.concatenate([near_ref[j, :, depth], far_ref[j, :, depth]], axis=0)
            total = total + lax.dot_general(
                gated[core], weight, (((1,), (1,)), ((), ())), preferred_element_type=F32
            )
        out_ref[j] = total.astype(BF16).reshape(out_ref.shape[1:])


def sum_kernel(where_ref, parts_ref, out_ref):
    groups, low, cores, rows, width = parts_ref.shape
    own_high = where_ref[2]
    unit = width // 2
    for x_low in range(low):
        totals = []
        for core in range(cores):
            total = parts_ref[0, x_low, core].astype(F32)
            for j in range(1, groups):
                total = total + parts_ref[j, x_low, core].astype(F32)
            totals.append(total)
        for far in range(2):
            high = own_high if far == 0 else 1 - own_high
            place = pl.multiple_of((high * low + x_low) * (cores * unit), cores * unit)
            pieces = [total[:, far * unit : (far + 1) * unit] for total in totals]
            columns = jnp.concatenate(pieces, axis=1)
            out_ref[:, pl.ds(place, cores * unit)] = columns.astype(BF16)


def exchange(x, axes):
    return lax.all_to_all(x, axes, 0, 0, tiled=True)


def body(gate_input, key_input, value_input, decay_rate, residue, skip_gain, out_weight):
    rows, width = key_input.shape
    modes = decay_rate.shape[0]
    z_size, high_size, low_size, cores = (lax.axis_size(a) for a in SEQ)
    y_size = lax.axis_size("chan")
    out_cols = out_weight.shape[1]
    chunks = z_size * high_size
    blocks = low_size * cores
    half = width // cores
    where = jnp.stack(
        [lax.axis_index(("z", "xh")), lax.axis_index("core"), lax.axis_index("xh")]
    ).astype(jnp.int32)

    own_weight = jnp.broadcast_to(out_weight.T[None], (z_size, out_cols, width))
    near = exchange(own_weight, "z")
    inputs = jnp.stack([key_input, value_input, gate_input])
    inputs = lax.all_gather(lax.all_gather(inputs, "xl"), "core")
    base, before, state, amplitude, rate = pl.pallas_call(
        chunk_kernel,
        out_shape=(
            jax.ShapeDtypeStruct((blocks, rows, half), F32),
            jax.ShapeDtypeStruct((blocks, modes, half), F32),
            jax.ShapeDtypeStruct((chunks, modes, half), F32),
            jax.ShapeDtypeStruct((modes, half), F32),
            jax.ShapeDtypeStruct((modes, half), F32),
        ),
        in_specs=[SMEM] + [VMEM] * 4,
        out_specs=(VMEM,) * 5,
        scratch_shapes=[
            pltpu.VMEM((blocks, rows, LANES), F32),
            pltpu.VMEM((blocks, modes, LANES), F32),
        ],
        compiler_params=PARAMS,
        name="chunk",
    )(where, inputs, decay_rate, residue, skip_gain[None, :])
    state, near = lax.optimization_barrier((state, near))
    far = lax.ppermute(near, "xh", [(0, 1), (1, 0)])
    states = exchange(state, ("z", "xh"))
    gated = pl.pallas_call(
        gate_kernel,
        out_shape=jax.ShapeDtypeStruct((blocks, rows, half), BF16),
        in_specs=[SMEM] + [VMEM] * 6,
        out_specs=VMEM,
        compiler_params=PARAMS,
        name="gate",
    )(where, states, before, rate, amplitude, base, inputs)
    gated, far = lax.optimization_barrier((gated, far))
    gated = lax.all_gather(gated, "core")
    piece = (rows, high_size * out_cols)
    parts = pl.pallas_call(
        project_kernel,
        out_shape=jax.ShapeDtypeStruct((y_size, blocks) + piece, BF16),
        in_specs=[VMEM] * 3,
        out_specs=VMEM,
        compiler_params=PARAMS,
        name="project",
    )(gated, near, far)
    parts = exchange(parts.reshape((y_size * blocks,) + piece), ("chan", "xl", "core"))
    return pl.pallas_call(
        sum_kernel,
        out_shape=jax.ShapeDtypeStruct((rows, width), BF16),
        in_specs=[SMEM, VMEM],
        out_specs=VMEM,
        compiler_params=PARAMS,
        name="sum_parts",
    )(where, parts.reshape((y_size, low_size, cores) + piece))


def solution(mesh):
    finer = Mesh(mesh.devices.reshape(8, 2, 2, 2, 8), SEQ + ("chan",))
    return jax.shard_map(
        body,
        mesh=finer,
        in_specs=(
            P(SEQ, "chan"),
            P(SEQ, "chan"),
            P(SEQ, "chan"),
            P(None, "chan"),
            P(None, "chan"),
            P("chan"),
            P("chan", SEQ),
        ),
        out_specs=P(SEQ, "chan"),
        check_vma=False,
    )
```

```python
import jax
import jax.numpy as jnp
from jax import lax
from jax.experimental import pallas as pl
from jax.experimental.pallas import tpu as pltpu
from jax.sharding import Mesh
from jax.sharding import PartitionSpec as P

F32 = jnp.float32
BF16 = jnp.bfloat16
SEQ = ("zh", "zl", "xh", "xl", "core")
LANES = 128
VMEM = pl.BlockSpec(memory_space=pltpu.VMEM)
SMEM = pl.BlockSpec(memory_space=pltpu.SMEM)
PARAMS = pltpu.CompilerParams(vmem_limit_bytes=48 * 1024 * 1024)


def tile_rows():
    return lax.broadcasted_iota(jnp.int32, (8, LANES), 0).astype(F32)


def chunk_kernel(
    where_ref, inputs_ref, rate_ref, residue_ref, skip_ref,
    base_ref, before_ref, send_ref, amp_ref, copy_ref, signal_ref, state_ref,
):
    blocks, rows, width = base_ref.shape
    modes = rate_ref.shape[0]
    tiles = rows // 8
    cores = inputs_ref.shape[0]
    first_col = where_ref[1] * width

    def slab(index, carry):
        cols = pl.ds(pl.multiple_of(index * LANES, LANES), LANES)
        source = pl.ds(pl.multiple_of(first_col + index * LANES, LANES), LANES)
        for i in range(blocks):
            key = inputs_ref[i % cores, i // cores, 0, :, source].astype(F32)
            signal_ref[i] = key * inputs_ref[i % cores, i // cores, 1, :, source].astype(F32)
        rate = rate_ref[:, source]
        amp = residue_ref[:, source] * jnp.sqrt(1.0 - jnp.exp(-2.0 * rate))
        amp_ref[:, cols] = amp
        copy_ref[:, cols] = rate
        steps = [jnp.exp(-8.0 * j * rate) for j in range(tiles)]
        scaled = [amp * step for step in steps]
        first = tile_rows()
        taps = [jnp.zeros((8, LANES), F32) for _ in range(tiles)]
        for m in range(modes):
            ahead = jnp.exp(-rate[m : m + 1] * first)
            behind = jnp.exp(-rate[m : m + 1] * (7.0 - first))
            held = [jnp.zeros((8, LANES), F32) for _ in range(blocks)]
            for j in range(tiles):
                taps[j] = taps[j] + scaled[j][m : m + 1] * ahead
                step = steps[tiles - 1 - j][m : m + 1]
                for i in range(blocks):
                    held[i] = held[i] + step * signal_ref[i, 8 * j : 8 * j + 8]
            for i in range(blocks):
                state_ref[i, m : m + 1] = jnp.sum(held[i] * behind, axis=0, keepdims=True)
        decay = jnp.exp(-float(rows) * rate)
        running = jnp.zeros((modes, LANES), F32)
        for i in range(blocks):
            before_ref[i, :, cols] = running
            running = decay * running + state_ref[i]
        for copy in range(send_ref.shape[0]):
            send_ref[copy, :, cols] = running
        row_ids = lax.broadcasted_iota(jnp.int32, (rows, LANES), 0)
        skip = skip_ref[0:1, source]

        def block(i, inner):
            signal = signal_ref[i]
            totals = [skip * signal[8 * j : 8 * j + 8] for j in range(tiles)]
            for lag in range(8):
                moved = signal
                if lag:
                    moved = jnp.where(row_ids >= lag, pltpu.roll(signal, lag, 0), 0.0)
                for j in range(tiles):
                    tap = taps[j][lag : lag + 1]
                    for k in range(j, tiles):
                        totals[k] = totals[k] + tap * moved[8 * (k - j) : 8 * (k - j) + 8]
            for j in range(tiles):
                base_ref[i, 8 * j : 8 * j + 8, cols] = totals[j]
            return inner

        return lax.fori_loop(0, blocks, block, carry)

    lax.fori_loop(0, width // LANES, slab, 0)


def gate_kernel(
    where_ref, chunks_ref, before_ref, rate_ref, amp_ref, base_ref, inputs_ref, gated_ref
):
    blocks, rows, width = base_ref.shape
    modes = rate_ref.shape[0]
    tiles = rows // 8
    cores = inputs_ref.shape[0]
    own = where_ref[0]
    first_col = where_ref[1] * width

    def slab(index, carry):
        cols = pl.ds(pl.multiple_of(index * LANES, LANES), LANES)
        source = pl.ds(pl.multiple_of(first_col + index * LANES, LANES), LANES)
        rate = rate_ref[:, cols]
        amp = amp_ref[:, cols]
        decay = jnp.exp(-float(rows * blocks) * rate)
        running = jnp.zeros((modes, LANES), F32)
        entering = jnp.zeros((modes, LANES), F32)
        for chunk in range(chunks_ref.shape[0]):
            entering = jnp.where(own == chunk, running, entering)
            running = decay * running + chunks_ref[chunk, :, cols]
        steps = [jnp.exp(-8.0 * j * rate) for j in range(tiles)]
        first = tile_rows() + 1.0
        aheads = [jnp.exp(-rate[m : m + 1] * first) for m in range(modes)]
        state = entering
        for i in range(blocks):
            full = (before_ref[i, :, cols] + state) * amp
            if i < blocks - 1:
                state = state * jnp.exp(-float(rows) * rate)
            parts = []
            for j in range(tiles):
                part = base_ref[i, 8 * j : 8 * j + 8, cols]
                scaled = full * steps[j]
                for m in range(modes):
                    part = part + scaled[m : m + 1] * aheads[m]
                parts.append(part)
            gate = inputs_ref[i % cores, i // cores, 2, :, source].astype(F32)
            gated_ref[i, :, cols] = (gate * jnp.concatenate(parts, axis=0)).astype(BF16)
        return carry

    lax.fori_loop(0, width // LANES, slab, 0)


def project_kernel(where_ref, gated_ref, weight_ref, other_ref, out_ref):
    own_low = where_ref[3]
    cores, shared, rows, half = gated_ref.shape
    gated = [gated_ref[core].reshape(shared * rows, half) for core in range(cores)]
    for ref, low in ((weight_ref, own_low), (other_ref, 1 - own_low)):
        for j in range(ref.shape[1]):
            total = 0.0
            for core in range(cores):
                depth = slice(core * half, (core + 1) * half)
                weight = jnp.concatenate([ref[i, j, :, depth] for i in range(2)], axis=0)
                total = total + lax.dot_general(
                    gated[core], weight, (((1,), (1,)), ((), ())), preferred_element_type=F32
                )
            out_ref[2 * j + low] = total.astype(BF16).reshape(out_ref.shape[1:])


def sum_kernel(where_ref, parts_ref, out_ref):
    groups, low, cores, rows, width = parts_ref.shape
    own_high = where_ref[2]
    unit = width // 2
    for x_low in range(low):
        totals = []
        for core in range(cores):
            total = parts_ref[0, x_low, core].astype(F32)
            for j in range(1, groups):
                total = total + parts_ref[j, x_low, core].astype(F32)
            totals.append(total)
        for far in range(2):
            high = own_high if far == 0 else 1 - own_high
            place = pl.multiple_of((high * low + x_low) * (cores * unit), cores * unit)
            pieces = [total[:, far * unit : (far + 1) * unit] for total in totals]
            columns = jnp.concatenate(pieces, axis=1)
            out_ref[:, pl.ds(place, cores * unit)] = columns.astype(BF16)


def exchange(x, axes):
    return lax.all_to_all(x, axes, 0, 0, tiled=True)


def body(gate_input, key_input, value_input, decay_rate, residue, skip_gain, out_weight):
    rows, width = key_input.shape
    modes = decay_rate.shape[0]
    zh_size, zl_size, high_size, low_size, cores = (lax.axis_size(a) for a in SEQ)
    y_size = lax.axis_size("chan")
    out_cols = out_weight.shape[1]
    chunks = zh_size * zl_size * high_size
    blocks = low_size * cores
    half = width // cores
    where = jnp.stack(
        [
            lax.axis_index(("zh", "zl", "xh")),
            lax.axis_index("core"),
            lax.axis_index("xh"),
            lax.axis_index("zl"),
        ]
    ).astype(jnp.int32)

    own_weight = jnp.broadcast_to(out_weight.T[None], (zh_size, out_cols, width))
    weight = exchange(own_weight, "zh")
    inputs = lax.all_gather(jnp.stack([key_input, value_input, gate_input]), "xl")
    inputs, weight = lax.optimization_barrier((inputs, weight))
    far = lax.ppermute(weight, "xh", [(0, 1), (1, 0)])
    inputs = lax.all_gather(inputs, "core")
    base, before, state, amplitude, rate = pl.pallas_call(
        chunk_kernel,
        out_shape=(
            jax.ShapeDtypeStruct((blocks, rows, half), F32),
            jax.ShapeDtypeStruct((blocks, modes, half), F32),
            jax.ShapeDtypeStruct((chunks, modes, half), F32),
            jax.ShapeDtypeStruct((modes, half), F32),
            jax.ShapeDtypeStruct((modes, half), F32),
        ),
        in_specs=[SMEM] + [VMEM] * 4,
        out_specs=(VMEM,) * 5,
        scratch_shapes=[
            pltpu.VMEM((blocks, rows, LANES), F32),
            pltpu.VMEM((blocks, modes, LANES), F32),
        ],
        compiler_params=PARAMS,
        name="chunk",
    )(where, inputs, decay_rate, residue, skip_gain[None, :])
    state, weight, far = lax.optimization_barrier((state, weight, far))
    weight = jnp.stack([weight, far])
    other = lax.ppermute(weight, "zl", [(0, 1), (1, 0)])
    states = exchange(state, ("zh", "zl", "xh"))
    gated = pl.pallas_call(
        gate_kernel,
        out_shape=jax.ShapeDtypeStruct((blocks, rows, half), BF16),
        in_specs=[SMEM] + [VMEM] * 6,
        out_specs=VMEM,
        compiler_params=PARAMS,
        name="gate",
    )(where, states, before, rate, amplitude, base, inputs)
    gated = lax.all_gather(gated, "core")
    piece = (rows, high_size * out_cols)
    parts = pl.pallas_call(
        project_kernel,
        out_shape=jax.ShapeDtypeStruct((y_size, blocks) + piece, BF16),
        in_specs=[SMEM] + [VMEM] * 3,
        out_specs=VMEM,
        compiler_params=PARAMS,
        name="project",
    )(where, gated, weight, other)
    parts = exchange(parts.reshape((y_size * blocks,) + piece), ("chan", "xl", "core"))
    return pl.pallas_call(
        sum_kernel,
        out_shape=jax.ShapeDtypeStruct((rows, width), BF16),
        in_specs=[SMEM, VMEM],
        out_specs=VMEM,
        compiler_params=PARAMS,
        name="sum_parts",
    )(where, parts.reshape((y_size, low_size, cores) + piece))


def solution(mesh):
    finer = Mesh(mesh.devices.reshape(4, 2, 2, 2, 2, 8), SEQ + ("chan",))
    return jax.shard_map(
        body,
        mesh=finer,
        in_specs=(
            P(SEQ, "chan"),
            P(SEQ, "chan"),
            P(SEQ, "chan"),
            P(None, "chan"),
            P(None, "chan"),
            P("chan"),
            P("chan", SEQ),
        ),
        out_specs=P(SEQ, "chan"),
        check_vma=False,
    )
```

```python
import jax
import jax.numpy as jnp
from jax import lax
from jax.experimental import pallas as pl
from jax.experimental.pallas import tpu as pltpu
from jax.sharding import Mesh
from jax.sharding import PartitionSpec as P

F32 = jnp.float32
BF16 = jnp.bfloat16
SEQ = ("zh", "zl", "xh", "xl", "core")
LANES = 128
VMEM = pl.BlockSpec(memory_space=pltpu.VMEM)
SMEM = pl.BlockSpec(memory_space=pltpu.SMEM)
PARAMS = pltpu.CompilerParams(vmem_limit_bytes=48 * 1024 * 1024)


def tile_rows():
    return lax.broadcasted_iota(jnp.int32, (8, LANES), 0).astype(F32)


def chunk_kernel(
    where_ref, inputs_ref, rate_ref, residue_ref, skip_ref,
    base_ref, before_ref, send_ref, amp_ref, copy_ref, signal_ref, state_ref,
):
    blocks, rows, width = base_ref.shape
    modes = rate_ref.shape[0]
    tiles = rows // 8
    cores = inputs_ref.shape[0]
    first_col = where_ref[1] * width

    def slab(index, carry):
        cols = pl.ds(pl.multiple_of(index * LANES, LANES), LANES)
        source = pl.ds(pl.multiple_of(first_col + index * LANES, LANES), LANES)
        for i in range(blocks):
            key = inputs_ref[i % cores, i // cores, 0, :, source].astype(F32)
            signal_ref[i] = key * inputs_ref[i % cores, i // cores, 1, :, source].astype(F32)
        rate = rate_ref[:, source]
        amp = residue_ref[:, source] * jnp.sqrt(1.0 - jnp.exp(-2.0 * rate))
        amp_ref[:, cols] = amp
        copy_ref[:, cols] = rate
        steps = [jnp.exp(-8.0 * j * rate) for j in range(tiles)]
        scaled = [amp * step for step in steps]
        first = tile_rows()
        taps = [jnp.zeros((8, LANES), F32) for _ in range(tiles)]
        for m in range(modes):
            ahead = jnp.exp(-rate[m : m + 1] * first)
            behind = jnp.exp(-rate[m : m + 1] * (7.0 - first))
            held = [jnp.zeros((8, LANES), F32) for _ in range(blocks)]
            for j in range(tiles):
                taps[j] = taps[j] + scaled[j][m : m + 1] * ahead
                step = steps[tiles - 1 - j][m : m + 1]
                for i in range(blocks):
                    held[i] = held[i] + step * signal_ref[i, 8 * j : 8 * j + 8]
            for i in range(blocks):
                state_ref[i, m : m + 1] = jnp.sum(held[i] * behind, axis=0, keepdims=True)
        decay = jnp.exp(-float(rows) * rate)
        running = jnp.zeros((modes, LANES), F32)
        for i in range(blocks):
            before_ref[i, :, cols] = running
            running = decay * running + state_ref[i]
        for copy in range(send_ref.shape[0]):
            send_ref[copy, :, cols] = running
        row_ids = lax.broadcasted_iota(jnp.int32, (rows, LANES), 0)
        skip = skip_ref[0:1, source]

        def block(i, inner):
            signal = signal_ref[i]
            totals = [skip * signal[8 * j : 8 * j + 8] for j in range(tiles)]
            for lag in range(8):
                moved = signal
                if lag:
                    moved = jnp.where(row_ids >= lag, pltpu.roll(signal, lag, 0), 0.0)
                for j in range(tiles):
                    tap = taps[j][lag : lag + 1]
                    for k in range(j, tiles):
                        totals[k] = totals[k] + tap * moved[8 * (k - j) : 8 * (k - j) + 8]
            for j in range(tiles):
                base_ref[i, 8 * j : 8 * j + 8, cols] = totals[j]
            return inner

        return lax.fori_loop(0, blocks, block, carry)

    lax.fori_loop(0, width // LANES, slab, 0)


def gate_kernel(
    where_ref, chunks_ref, before_ref, rate_ref, amp_ref, base_ref, inputs_ref, gated_ref
):
    blocks, rows, width = base_ref.shape
    modes = rate_ref.shape[0]
    tiles = rows // 8
    cores = inputs_ref.shape[0]
    own = where_ref[0]
    first_col = where_ref[1] * width

    def slab(index, carry):
        cols = pl.ds(pl.multiple_of(index * LANES, LANES), LANES)
        source = pl.ds(pl.multiple_of(first_col + index * LANES, LANES), LANES)
        rate = rate_ref[:, cols]
        amp = amp_ref[:, cols]
        decay = jnp.exp(-float(rows * blocks) * rate)
        running = jnp.zeros((modes, LANES), F32)
        entering = jnp.zeros((modes, LANES), F32)
        for chunk in range(chunks_ref.shape[0]):
            entering = jnp.where(own == chunk, running, entering)
            running = decay * running + chunks_ref[chunk, :, cols]
        steps = [jnp.exp(-8.0 * j * rate) for j in range(tiles)]
        first = tile_rows() + 1.0
        aheads = [jnp.exp(-rate[m : m + 1] * first) for m in range(modes)]
        state = entering
        for i in range(blocks):
            full = (before_ref[i, :, cols] + state) * amp
            if i < blocks - 1:
                state = state * jnp.exp(-float(rows) * rate)
            parts = []
            for j in range(tiles):
                part = base_ref[i, 8 * j : 8 * j + 8, cols]
                scaled = full * steps[j]
                for m in range(modes):
                    part = part + scaled[m : m + 1] * aheads[m]
                parts.append(part)
            gate = inputs_ref[i % cores, i // cores, 2, :, source].astype(F32)
            gated_ref[i, :, cols] = (gate * jnp.concatenate(parts, axis=0)).astype(BF16)
        return carry

    lax.fori_loop(0, width // LANES, slab, 0)


def project_kernel(where_ref, gated_ref, own_ref, x_ref, z_ref, both_ref, out_ref):
    own_low = where_ref[3]
    cores, shared, rows, half = gated_ref.shape
    gated = [gated_ref[core].reshape(shared * rows, half) for core in range(cores)]
    for refs, low in (((own_ref, x_ref), own_low), ((z_ref, both_ref), 1 - own_low)):
        for j in range(own_ref.shape[0]):
            total = 0.0
            for core in range(cores):
                depth = slice(core * half, (core + 1) * half)
                weight = jnp.concatenate([ref[j, :, depth] for ref in refs], axis=0)
                total = total + lax.dot_general(
                    gated[core], weight, (((1,), (1,)), ((), ())), preferred_element_type=F32
                )
            out_ref[2 * j + low] = total.astype(BF16).reshape(out_ref.shape[1:])


def sum_kernel(where_ref, parts_ref, out_ref):
    groups, low, cores, rows, width = parts_ref.shape
    own_high = where_ref[2]
    unit = width // 2
    for x_low in range(low):
        totals = []
        for core in range(cores):
            total = parts_ref[0, x_low, core].astype(F32)
            for j in range(1, groups):
                total = total + parts_ref[j, x_low, core].astype(F32)
            totals.append(total)
        for far in range(2):
            high = own_high if far == 0 else 1 - own_high
            place = pl.multiple_of((high * low + x_low) * (cores * unit), cores * unit)
            pieces = [total[:, far * unit : (far + 1) * unit] for total in totals]
            columns = jnp.concatenate(pieces, axis=1)
            out_ref[:, pl.ds(place, cores * unit)] = columns.astype(BF16)


def exchange(x, axes):
    return lax.all_to_all(x, axes, 0, 0, tiled=True)


def body(gate_input, key_input, value_input, decay_rate, residue, skip_gain, out_weight):
    rows, width = key_input.shape
    modes = decay_rate.shape[0]
    zh_size, zl_size, high_size, low_size, cores = (lax.axis_size(a) for a in SEQ)
    y_size = lax.axis_size("chan")
    out_cols = out_weight.shape[1]
    chunks = zh_size * zl_size * high_size
    blocks = low_size * cores
    half = width // cores
    where = jnp.stack(
        [
            lax.axis_index(("zh", "zl", "xh")),
            lax.axis_index("core"),
            lax.axis_index("xh"),
            lax.axis_index("zl"),
        ]
    ).astype(jnp.int32)

    own_weight = jnp.broadcast_to(out_weight.T[None], (zh_size, out_cols, width))
    weight = exchange(own_weight, "zh")
    inputs = lax.all_gather(jnp.stack([key_input, value_input, gate_input]), "xl")
    inputs = lax.all_gather(inputs, "core")
    base, before, state, amplitude, rate = pl.pallas_call(
        chunk_kernel,
        out_shape=(
            jax.ShapeDtypeStruct((blocks, rows, half), F32),
            jax.ShapeDtypeStruct((blocks, modes, half), F32),
            jax.ShapeDtypeStruct((chunks, modes, half), F32),
            jax.ShapeDtypeStruct((modes, half), F32),
            jax.ShapeDtypeStruct((modes, half), F32),
        ),
        in_specs=[SMEM] + [VMEM] * 4,
        out_specs=(VMEM,) * 5,
        scratch_shapes=[
            pltpu.VMEM((blocks, rows, LANES), F32),
            pltpu.VMEM((blocks, modes, LANES), F32),
        ],
        compiler_params=PARAMS,
        name="chunk",
    )(where, inputs, decay_rate, residue, skip_gain[None, :])
    state, weight = lax.optimization_barrier((state, weight))
    swap, cross = [(0, 1), (1, 0)], [(0, 3), (1, 2), (2, 1), (3, 0)]
    weights = (
        weight,
        lax.ppermute(weight, "xh", swap),
        lax.ppermute(weight, "zl", swap),
        lax.ppermute(weight, ("zl", "xh"), cross),
    )
    states = exchange(state, ("zh", "zl", "xh"))
    gated = pl.pallas_call(
        gate_kernel,
        out_shape=jax.ShapeDtypeStruct((blocks, rows, half), BF16),
        in_specs=[SMEM] + [VMEM] * 6,
        out_specs=VMEM,
        compiler_params=PARAMS,
        name="gate",
    )(where, states, before, rate, amplitude, base, inputs)
    gated = lax.all_gather(gated, "core")
    piece = (rows, high_size * out_cols)
    parts = pl.pallas_call(
        project_kernel,
        out_shape=jax.ShapeDtypeStruct((y_size, blocks) + piece, BF16),
        in_specs=[SMEM] + [VMEM] * 5,
        out_specs=VMEM,
        compiler_params=PARAMS,
        name="project",
    )(where, gated, *weights)
    parts = exchange(parts.reshape((y_size * blocks,) + piece), ("chan", "xl", "core"))
    return pl.pallas_call(
        sum_kernel,
        out_shape=jax.ShapeDtypeStruct((rows, width), BF16),
        in_specs=[SMEM, VMEM],
        out_specs=VMEM,
        compiler_params=PARAMS,
        name="sum_parts",
    )(where, parts.reshape((y_size, low_size, cores) + piece))


def solution(mesh):
    finer = Mesh(mesh.devices.reshape(4, 2, 2, 2, 2, 8), SEQ + ("chan",))
    return jax.shard_map(
        body,
        mesh=finer,
        in_specs=(
            P(SEQ, "chan"),
            P(SEQ, "chan"),
            P(SEQ, "chan"),
            P(None, "chan"),
            P(None, "chan"),
            P("chan"),
            P("chan", SEQ),
        ),
        out_specs=P(SEQ, "chan"),
        check_vma=False,
    )
```

```python
import jax
import jax.numpy as jnp
from jax import lax
from jax.experimental import pallas as pl
from jax.experimental.pallas import tpu as pltpu
from jax.sharding import Mesh
from jax.sharding import PartitionSpec as P

F32 = jnp.float32
BF16 = jnp.bfloat16
SEQ = ("zh", "zl", "xh", "xl", "core")
LANES = 128
VMEM = pl.BlockSpec(memory_space=pltpu.VMEM)
SMEM = pl.BlockSpec(memory_space=pltpu.SMEM)
PARAMS = pltpu.CompilerParams(vmem_limit_bytes=48 * 1024 * 1024)


def tile_rows():
    return lax.broadcasted_iota(jnp.int32, (8, LANES), 0).astype(F32)


def chunk_kernel(
    where_ref, inputs_ref, rate_ref, residue_ref, skip_ref,
    base_ref, before_ref, send_ref, amp_ref, copy_ref, signal_ref, state_ref,
):
    blocks, rows, width = base_ref.shape
    modes = rate_ref.shape[0]
    tiles = rows // 8
    cores = inputs_ref.shape[0]
    first_col = where_ref[1] * width

    def slab(index, carry):
        cols = pl.ds(pl.multiple_of(index * LANES, LANES), LANES)
        source = pl.ds(pl.multiple_of(first_col + index * LANES, LANES), LANES)
        for i in range(blocks):
            key = inputs_ref[i % cores, i // cores, 0, :, source].astype(F32)
            signal_ref[i] = key * inputs_ref[i % cores, i // cores, 1, :, source].astype(F32)
        rate = rate_ref[:, source]
        amp = residue_ref[:, source] * jnp.sqrt(1.0 - jnp.exp(-2.0 * rate))
        amp_ref[:, cols] = amp
        copy_ref[:, cols] = rate
        steps = [jnp.exp(-8.0 * j * rate) for j in range(tiles)]
        scaled = [amp * step for step in steps]
        first = tile_rows()
        taps = [jnp.zeros((8, LANES), F32) for _ in range(tiles)]
        for m in range(modes):
            ahead = jnp.exp(-rate[m : m + 1] * first)
            behind = jnp.exp(-rate[m : m + 1] * (7.0 - first))
            held = [jnp.zeros((8, LANES), F32) for _ in range(blocks)]
            for j in range(tiles):
                taps[j] = taps[j] + scaled[j][m : m + 1] * ahead
                step = steps[tiles - 1 - j][m : m + 1]
                for i in range(blocks):
                    held[i] = held[i] + step * signal_ref[i, 8 * j : 8 * j + 8]
            for i in range(blocks):
                state_ref[i, m : m + 1] = jnp.sum(held[i] * behind, axis=0, keepdims=True)
        decay = jnp.exp(-float(rows) * rate)
        running = jnp.zeros((modes, LANES), F32)
        for i in range(blocks):
            before_ref[i, :, cols] = running
            running = decay * running + state_ref[i]
        for copy in range(send_ref.shape[0]):
            send_ref[copy, :, cols] = running
        row_ids = lax.broadcasted_iota(jnp.int32, (rows, LANES), 0)
        skip = skip_ref[0:1, source]

        def block(i, inner):
            signal = signal_ref[i]
            totals = [skip * signal[8 * j : 8 * j + 8] for j in range(tiles)]
            for lag in range(8):
                moved = signal
                if lag:
                    moved = jnp.where(row_ids >= lag, pltpu.roll(signal, lag, 0), 0.0)
                for j in range(tiles):
                    tap = taps[j][lag : lag + 1]
                    for k in range(j, tiles):
                        totals[k] = totals[k] + tap * moved[8 * (k - j) : 8 * (k - j) + 8]
            for j in range(tiles):
                base_ref[i, 8 * j : 8 * j + 8, cols] = totals[j]
            return inner

        return lax.fori_loop(0, blocks, block, carry)

    lax.fori_loop(0, width // LANES, slab, 0)


def gate_kernel(
    where_ref, chunks_ref, before_ref, rate_ref, amp_ref, base_ref, inputs_ref, gated_ref
):
    blocks, rows, width = base_ref.shape
    modes = rate_ref.shape[0]
    tiles = rows // 8
    cores = inputs_ref.shape[0]
    own = where_ref[0]
    first_col = where_ref[1] * width

    def slab(index, carry):
        cols = pl.ds(pl.multiple_of(index * LANES, LANES), LANES)
        source = pl.ds(pl.multiple_of(first_col + index * LANES, LANES), LANES)
        rate = rate_ref[:, cols]
        amp = amp_ref[:, cols]
        decay = jnp.exp(-float(rows * blocks) * rate)
        running = jnp.zeros((modes, LANES), F32)
        entering = jnp.zeros((modes, LANES), F32)
        for chunk in range(chunks_ref.shape[0]):
            entering = jnp.where(own == chunk, running, entering)
            running = decay * running + chunks_ref[chunk, :, cols]
        steps = [jnp.exp(-8.0 * j * rate) for j in range(tiles)]
        first = tile_rows() + 1.0
        aheads = [jnp.exp(-rate[m : m + 1] * first) for m in range(modes)]
        state = entering
        for i in range(blocks):
            full = (before_ref[i, :, cols] + state) * amp
            if i < blocks - 1:
                state = state * jnp.exp(-float(rows) * rate)
            parts = []
            for j in range(tiles):
                part = base_ref[i, 8 * j : 8 * j + 8, cols]
                scaled = full * steps[j]
                for m in range(modes):
                    part = part + scaled[m : m + 1] * aheads[m]
                parts.append(part)
            gate = inputs_ref[i % cores, i // cores, 2, :, source].astype(F32)
            gated_ref[i, :, cols] = (gate * jnp.concatenate(parts, axis=0)).astype(BF16)
        return carry

    lax.fori_loop(0, width // LANES, slab, 0)


def project_kernel(where_ref, gated_ref, own_ref, below_ref, above_ref, out_ref):
    own_low = where_ref[2]
    cores, shared, rows, half = gated_ref.shape
    gated = [gated_ref[core].reshape(shared * rows, half) for core in range(cores)]
    split = below_ref.shape[0]

    def columns(ref, j, place):
        total = 0.0
        for core in range(cores):
            depth = slice(core * half, (core + 1) * half)
            weight = jnp.concatenate([ref[j, i, :, depth] for i in range(ref.shape[1])], axis=0)
            total = total + lax.dot_general(
                gated[core], weight, (((1,), (1,)), ((), ())), preferred_element_type=F32
            )
        out_ref[place] = total.astype(BF16).reshape(out_ref.shape[1:])

    for j in range(own_ref.shape[0]):
        columns(own_ref, j, 2 * j + own_low)
    for j in range(split):
        columns(below_ref, j, 2 * j + 1 - own_low)
        columns(above_ref, j, 2 * (split + j) + 1 - own_low)


def sum_kernel(parts_ref, out_ref):
    groups, low, cores, rows, width = parts_ref.shape
    unit = width // 2
    for x_low in range(low):
        totals = []
        for core in range(cores):
            total = parts_ref[0, x_low, core].astype(F32)
            for j in range(1, groups):
                total = total + parts_ref[j, x_low, core].astype(F32)
            totals.append(total)
        for high in range(width // unit):
            place = (high * low + x_low) * (cores * unit)
            pieces = [total[:, high * unit : (high + 1) * unit] for total in totals]
            columns = jnp.concatenate(pieces, axis=1)
            out_ref[:, place : place + cores * unit] = columns.astype(BF16)


def exchange(x, axes):
    return lax.all_to_all(x, axes, 0, 0, tiled=True)


def body(gate_input, key_input, value_input, decay_rate, residue, skip_gain, out_weight):
    rows, width = key_input.shape
    modes = decay_rate.shape[0]
    zh_size, zl_size, high_size, low_size, cores = (lax.axis_size(a) for a in SEQ)
    y_size = lax.axis_size("chan")
    out_cols = out_weight.shape[1]
    chunks = zh_size * zl_size * high_size
    blocks = low_size * cores
    half = width // cores
    where = jnp.stack(
        [
            lax.axis_index(("zh", "zl", "xh")),
            lax.axis_index("core"),
            lax.axis_index("zl"),
        ]
    ).astype(jnp.int32)

    own_weight = jnp.broadcast_to(
        out_weight.T[None, None], (zh_size, high_size, out_cols, width)
    )
    weight = exchange(own_weight.reshape(-1, out_cols, width), ("zh", "xh"))
    weight = weight.reshape(own_weight.shape)
    inputs = lax.all_gather(jnp.stack([key_input, value_input, gate_input]), "xl")
    inputs = lax.all_gather(inputs, "core")
    base, before, state, amplitude, rate = pl.pallas_call(
        chunk_kernel,
        out_shape=(
            jax.ShapeDtypeStruct((blocks, rows, half), F32),
            jax.ShapeDtypeStruct((blocks, modes, half), F32),
            jax.ShapeDtypeStruct((chunks, modes, half), F32),
            jax.ShapeDtypeStruct((modes, half), F32),
            jax.ShapeDtypeStruct((modes, half), F32),
        ),
        in_specs=[SMEM] + [VMEM] * 4,
        out_specs=(VMEM,) * 5,
        scratch_shapes=[
            pltpu.VMEM((blocks, rows, LANES), F32),
            pltpu.VMEM((blocks, modes, LANES), F32),
        ],
        compiler_params=PARAMS,
        name="chunk",
    )(where, inputs, decay_rate, residue, skip_gain[None, :])
    state, weight = lax.optimization_barrier((state, weight))
    ring = zh_size * zl_size
    up = [(i, (i + 1) % ring) for i in range(ring)]
    down = [(i, (i + ring - 1) % ring) for i in range(ring)]
    split = zh_size // 2
    weights = (
        weight,
        lax.ppermute(weight[:split], ("zh", "zl"), up),
        lax.ppermute(weight[split:], ("zh", "zl"), down),
    )
    states = exchange(state, ("zh", "zl", "xh"))
    gated = pl.pallas_call(
        gate_kernel,
        out_shape=jax.ShapeDtypeStruct((blocks, rows, half), BF16),
        in_specs=[SMEM] + [VMEM] * 6,
        out_specs=VMEM,
        compiler_params=PARAMS,
        name="gate",
    )(where, states, before, rate, amplitude, base, inputs)
    gated = lax.all_gather(gated, "core")
    piece = (rows, high_size * out_cols)
    parts = pl.pallas_call(
        project_kernel,
        out_shape=jax.ShapeDtypeStruct((y_size, blocks) + piece, BF16),
        in_specs=[SMEM] + [VMEM] * 4,
        out_specs=VMEM,
        compiler_params=PARAMS,
        name="project",
    )(where, gated, *weights)
    parts = exchange(parts.reshape((y_size * blocks,) + piece), ("chan", "xl", "core"))
    return pl.pallas_call(
        sum_kernel,
        out_shape=jax.ShapeDtypeStruct((rows, width), BF16),
        in_specs=[VMEM],
        out_specs=VMEM,
        compiler_params=PARAMS,
        name="sum_parts",
    )(parts.reshape((y_size, low_size, cores) + piece))


def solution(mesh):
    finer = Mesh(mesh.devices.reshape(4, 2, 2, 2, 2, 8), SEQ + ("chan",))
    return jax.shard_map(
        body,
        mesh=finer,
        in_specs=(
            P(SEQ, "chan"),
            P(SEQ, "chan"),
            P(SEQ, "chan"),
            P(None, "chan"),
            P(None, "chan"),
            P("chan"),
            P("chan", SEQ),
        ),
        out_specs=P(SEQ, "chan"),
        check_vma=False,
    )
```

```python
import jax
import jax.numpy as jnp
from jax import lax
from jax.experimental import pallas as pl
from jax.experimental.pallas import tpu as pltpu
from jax.sharding import Mesh
from jax.sharding import PartitionSpec as P

F32 = jnp.float32
BF16 = jnp.bfloat16
SEQ = ("z", "xh", "xl", "core")
LANES = 128
VMEM = pl.BlockSpec(memory_space=pltpu.VMEM)
SMEM = pl.BlockSpec(memory_space=pltpu.SMEM)
PARAMS = pltpu.CompilerParams(vmem_limit_bytes=48 * 1024 * 1024)


def tile_rows():
    return lax.broadcasted_iota(jnp.int32, (8, LANES), 0).astype(F32)


def copies_kernel(weight_ref, out_ref, sems):
    copies = [
        pltpu.make_async_copy(weight_ref, out_ref.at[i], sems.at[i])
        for i in range(out_ref.shape[0])
    ]
    for copy in copies:
        copy.start()
    for copy in copies:
        copy.wait()


def chunk_kernel(
    where_ref, inputs_ref, rate_ref, residue_ref, skip_ref,
    base_ref, before_ref, send_ref, amp_ref, copy_ref, signal_ref, state_ref,
):
    blocks, rows, width = base_ref.shape
    modes = rate_ref.shape[0]
    tiles = rows // 8
    cores = inputs_ref.shape[0]
    first_col = where_ref[1] * width

    def slab(index, carry):
        cols = pl.ds(pl.multiple_of(index * LANES, LANES), LANES)
        source = pl.ds(pl.multiple_of(first_col + index * LANES, LANES), LANES)
        for i in range(blocks):
            key = inputs_ref[i % cores, i // cores, 0, :, source].astype(F32)
            signal_ref[i] = key * inputs_ref[i % cores, i // cores, 1, :, source].astype(F32)
        rate = rate_ref[:, source]
        amp = residue_ref[:, source] * jnp.sqrt(1.0 - jnp.exp(-2.0 * rate))
        amp_ref[:, cols] = amp
        copy_ref[:, cols] = rate
        steps = [jnp.exp(-8.0 * j * rate) for j in range(tiles)]
        scaled = [amp * step for step in steps]
        first = tile_rows()
        taps = [jnp.zeros((8, LANES), F32) for _ in range(tiles)]
        for m in range(modes):
            ahead = jnp.exp(-rate[m : m + 1] * first)
            behind = jnp.exp(-rate[m : m + 1] * (7.0 - first))
            held = [jnp.zeros((8, LANES), F32) for _ in range(blocks)]
            for j in range(tiles):
                taps[j] = taps[j] + scaled[j][m : m + 1] * ahead
                step = steps[tiles - 1 - j][m : m + 1]
                for i in range(blocks):
                    held[i] = held[i] + step * signal_ref[i, 8 * j : 8 * j + 8]
            for i in range(blocks):
                state_ref[i, m : m + 1] = jnp.sum(held[i] * behind, axis=0, keepdims=True)
        decay = jnp.exp(-float(rows) * rate)
        running = jnp.zeros((modes, LANES), F32)
        for i in range(blocks):
            before_ref[i, :, cols] = running
            running = decay * running + state_ref[i]
        for copy in range(send_ref.shape[0]):
            send_ref[copy, :, cols] = running
        row_ids = lax.broadcasted_iota(jnp.int32, (rows, LANES), 0)
        skip = skip_ref[0:1, source]

        def block(i, inner):
            signal = signal_ref[i]
            totals = [skip * signal[8 * j : 8 * j + 8] for j in range(tiles)]
            for lag in range(8):
                moved = signal
                if lag:
                    moved = jnp.where(row_ids >= lag, pltpu.roll(signal, lag, 0), 0.0)
                for j in range(tiles):
                    tap = taps[j][lag : lag + 1]
                    for k in range(j, tiles):
                        totals[k] = totals[k] + tap * moved[8 * (k - j) : 8 * (k - j) + 8]
            for j in range(tiles):
                base_ref[i, 8 * j : 8 * j + 8, cols] = totals[j]
            return inner

        return lax.fori_loop(0, blocks, block, carry)

    lax.fori_loop(0, width // LANES, slab, 0)


def gate_kernel(
    where_ref, chunks_ref, before_ref, rate_ref, amp_ref, base_ref, inputs_ref, gated_ref
):
    blocks, rows, width = base_ref.shape
    modes = rate_ref.shape[0]
    tiles = rows // 8
    cores = inputs_ref.shape[0]
    own = where_ref[0]
    first_col = where_ref[1] * width

    def slab(index, carry):
        cols = pl.ds(pl.multiple_of(index * LANES, LANES), LANES)
        source = pl.ds(pl.multiple_of(first_col + index * LANES, LANES), LANES)
        rate = rate_ref[:, cols]
        amp = amp_ref[:, cols]
        decay = jnp.exp(-float(rows * blocks) * rate)
        running = jnp.zeros((modes, LANES), F32)
        entering = jnp.zeros((modes, LANES), F32)
        for chunk in range(chunks_ref.shape[0]):
            entering = jnp.where(own == chunk, running, entering)
            running = decay * running + chunks_ref[chunk, :, cols]
        steps = [jnp.exp(-8.0 * j * rate) for j in range(tiles)]
        first = tile_rows() + 1.0
        aheads = [jnp.exp(-rate[m : m + 1] * first) for m in range(modes)]
        state = entering
        for i in range(blocks):
            full = (before_ref[i, :, cols] + state) * amp
            if i < blocks - 1:
                state = state * jnp.exp(-float(rows) * rate)
            parts = []
            for j in range(tiles):
                part = base_ref[i, 8 * j : 8 * j + 8, cols]
                scaled = full * steps[j]
                for m in range(modes):
                    part = part + scaled[m : m + 1] * aheads[m]
                parts.append(part)
            gate = inputs_ref[i % cores, i // cores, 2, :, source].astype(F32)
            gated_ref[i, :, cols] = (gate * jnp.concatenate(parts, axis=0)).astype(BF16)
        return carry

    lax.fori_loop(0, width // LANES, slab, 0)


def project_kernel(gated_ref, near_ref, far_ref, out_ref):
    cores, shared, rows, half = gated_ref.shape
    gated = [gated_ref[core].reshape(shared * rows, half) for core in range(cores)]
    for j in range(out_ref.shape[0]):
        total = 0.0
        for core in range(cores):
            depth = slice(core * half, (core + 1) * half)
            weight = jnp.concatenate([near_ref[j, :, depth], far_ref[j, :, depth]], axis=0)
            total = total + lax.dot_general(
                gated[core], weight, (((1,), (1,)), ((), ())), preferred_element_type=F32
            )
        out_ref[j] = total.astype(BF16).reshape(out_ref.shape[1:])


def sum_kernel(where_ref, parts_ref, out_ref):
    groups, low, cores, rows, width = parts_ref.shape
    own_high = where_ref[2]
    unit = width // 2
    for x_low in range(low):
        totals = []
        for core in range(cores):
            total = parts_ref[0, x_low, core].astype(F32)
            for j in range(1, groups):
                total = total + parts_ref[j, x_low, core].astype(F32)
            totals.append(total)
        near = [total[:, :unit] for total in totals]
        far = [total[:, unit:] for total in totals]
        near, far = jnp.concatenate(near, axis=1), jnp.concatenate(far, axis=1)
        for high in range(2):
            place = (high * low + x_low) * (cores * unit)
            columns = jnp.where(own_high == high, near, far)
            out_ref[:, place : place + cores * unit] = columns.astype(BF16)


def exchange(x, axes):
    return lax.all_to_all(x, axes, 0, 0, tiled=True)


def body(gate_input, key_input, value_input, decay_rate, residue, skip_gain, out_weight):
    rows, width = key_input.shape
    modes = decay_rate.shape[0]
    z_size, high_size, low_size, cores = (lax.axis_size(a) for a in SEQ)
    y_size = lax.axis_size("chan")
    out_cols = out_weight.shape[1]
    chunks = z_size * high_size
    blocks = low_size * cores
    half = width // cores
    where = jnp.stack(
        [lax.axis_index(("z", "xh")), lax.axis_index("core"), lax.axis_index("xh")]
    ).astype(jnp.int32)

    own_weight = pl.pallas_call(
        copies_kernel,
        out_shape=jax.ShapeDtypeStruct((z_size, out_cols, width), BF16),
        in_specs=[pl.BlockSpec(memory_space=pl.ANY)],
        out_specs=pl.BlockSpec(memory_space=pl.ANY),
        scratch_shapes=[pltpu.SemaphoreType.DMA((z_size,))],
        compiler_params=PARAMS,
        name="copies",
    )(out_weight.T)
    near = exchange(own_weight, "z")
    inputs = jnp.stack([key_input, value_input, gate_input])
    inputs = lax.all_gather(lax.all_gather(inputs, "xl"), "core")
    base, before, state, amplitude, rate = pl.pallas_call(
        chunk_kernel,
        out_shape=(
            jax.ShapeDtypeStruct((blocks, rows, half), F32),
            jax.ShapeDtypeStruct((blocks, modes, half), F32),
            jax.ShapeDtypeStruct((chunks, modes, half), F32),
            jax.ShapeDtypeStruct((modes, half), F32),
            jax.ShapeDtypeStruct((modes, half), F32),
        ),
        in_specs=[SMEM] + [VMEM] * 4,
        out_specs=(VMEM,) * 5,
        scratch_shapes=[
            pltpu.VMEM((blocks, rows, LANES), F32),
            pltpu.VMEM((blocks, modes, LANES), F32),
        ],
        compiler_params=PARAMS,
        name="chunk",
    )(where, inputs, decay_rate, residue, skip_gain[None, :])
    state, near = lax.optimization_barrier((state, near))
    far = lax.ppermute(near, "xh", [(0, 1), (1, 0)])
    states = exchange(state, ("z", "xh"))
    gated = pl.pallas_call(
        gate_kernel,
        out_shape=jax.ShapeDtypeStruct((blocks, rows, half), BF16),
        in_specs=[SMEM] + [VMEM] * 6,
        out_specs=VMEM,
        compiler_params=PARAMS,
        name="gate",
    )(where, states, before, rate, amplitude, base, inputs)
    gated, far = lax.optimization_barrier((gated, far))
    gated = lax.all_gather(gated, "core")
    piece = (rows, high_size * out_cols)
    parts = pl.pallas_call(
        project_kernel,
        out_shape=jax.ShapeDtypeStruct((y_size, blocks) + piece, BF16),
        in_specs=[VMEM] * 3,
        out_specs=VMEM,
        compiler_params=PARAMS,
        name="project",
    )(gated, near, far)
    parts = exchange(parts.reshape((y_size * blocks,) + piece), ("chan", "xl", "core"))
    return pl.pallas_call(
        sum_kernel,
        out_shape=jax.ShapeDtypeStruct((rows, width), BF16),
        in_specs=[SMEM, VMEM],
        out_specs=VMEM,
        compiler_params=PARAMS,
        name="sum_parts",
    )(where, parts.reshape((y_size, low_size, cores) + piece))


def solution(mesh):
    finer = Mesh(mesh.devices.reshape(8, 2, 2, 2, 8), SEQ + ("chan",))
    return jax.shard_map(
        body,
        mesh=finer,
        in_specs=(
            P(SEQ, "chan"),
            P(SEQ, "chan"),
            P(SEQ, "chan"),
            P(None, "chan"),
            P(None, "chan"),
            P("chan"),
            P("chan", SEQ),
        ),
        out_specs=P(SEQ, "chan"),
        check_vma=False,
    )
```

```python
import jax
import jax.numpy as jnp
from jax import lax
from jax.experimental import pallas as pl
from jax.experimental.pallas import tpu as pltpu
from jax.sharding import Mesh
from jax.sharding import PartitionSpec as P

F32 = jnp.float32
BF16 = jnp.bfloat16
SEQ = ("z", "xh", "xl", "core")
LANES = 128
VMEM = pl.BlockSpec(memory_space=pltpu.VMEM)
PARAMS = pltpu.CompilerParams(vmem_limit_bytes=48 * 1024 * 1024)


def tile_rows():
    return lax.broadcasted_iota(jnp.int32, (8, LANES), 0).astype(F32)


def chunk_kernel(
    inputs_ref, rate_ref, residue_ref, skip_ref,
    base_ref, before_ref, send_ref, amp_ref, copy_ref, signal_ref, state_ref,
):
    blocks, rows, width = base_ref.shape
    modes = rate_ref.shape[0]
    tiles = rows // 8
    cores = inputs_ref.shape[0]
    first_col = lax.axis_index("core") * width

    def slab(index, carry):
        cols = pl.ds(pl.multiple_of(index * LANES, LANES), LANES)
        source = pl.ds(pl.multiple_of(first_col + index * LANES, LANES), LANES)
        for i in range(blocks):
            key = inputs_ref[i % cores, i // cores, 0, :, source].astype(F32)
            signal_ref[i] = key * inputs_ref[i % cores, i // cores, 1, :, source].astype(F32)
        rate = rate_ref[:, source]
        amp = residue_ref[:, source] * jnp.sqrt(1.0 - jnp.exp(-2.0 * rate))
        amp_ref[:, cols] = amp
        copy_ref[:, cols] = rate
        steps = [jnp.exp(-8.0 * j * rate) for j in range(tiles)]
        scaled = [amp * step for step in steps]
        first = tile_rows()
        taps = [jnp.zeros((8, LANES), F32) for _ in range(tiles)]
        for m in range(modes):
            ahead = jnp.exp(-rate[m : m + 1] * first)
            behind = jnp.exp(-rate[m : m + 1] * (7.0 - first))
            held = [jnp.zeros((8, LANES), F32) for _ in range(blocks)]
            for j in range(tiles):
                taps[j] = taps[j] + scaled[j][m : m + 1] * ahead
                step = steps[tiles - 1 - j][m : m + 1]
                for i in range(blocks):
                    held[i] = held[i] + step * signal_ref[i, 8 * j : 8 * j + 8]
            for i in range(blocks):
                state_ref[i, m : m + 1] = jnp.sum(held[i] * behind, axis=0, keepdims=True)
        decay = jnp.exp(-float(rows) * rate)
        running = jnp.zeros((modes, LANES), F32)
        for i in range(blocks):
            before_ref[i, :, cols] = running
            running = decay * running + state_ref[i]
        for copy in range(send_ref.shape[0]):
            send_ref[copy, :, cols] = running
        row_ids = lax.broadcasted_iota(jnp.int32, (rows, LANES), 0)
        skip = skip_ref[0:1, source]

        def block(i, inner):
            signal = signal_ref[i]
            totals = [skip * signal[8 * j : 8 * j + 8] for j in range(tiles)]
            for lag in range(8):
                moved = signal
                if lag:
                    moved = jnp.where(row_ids >= lag, pltpu.roll(signal, lag, 0), 0.0)
                for j in range(tiles):
                    tap = taps[j][lag : lag + 1]
                    for k in range(j, tiles):
                        totals[k] = totals[k] + tap * moved[8 * (k - j) : 8 * (k - j) + 8]
            for j in range(tiles):
                base_ref[i, 8 * j : 8 * j + 8, cols] = totals[j]
            return inner

        return lax.fori_loop(0, blocks, block, carry)

    lax.fori_loop(0, width // LANES, slab, 0)


def gate_kernel(
    chunks_ref, before_ref, rate_ref, amp_ref, base_ref, inputs_ref, gated_ref
):
    blocks, rows, width = base_ref.shape
    modes = rate_ref.shape[0]
    tiles = rows // 8
    cores = inputs_ref.shape[0]
    own = lax.axis_index("z") * lax.axis_size("xh") + lax.axis_index("xh")
    first_col = lax.axis_index("core") * width

    def slab(index, carry):
        cols = pl.ds(pl.multiple_of(index * LANES, LANES), LANES)
        source = pl.ds(pl.multiple_of(first_col + index * LANES, LANES), LANES)
        rate = rate_ref[:, cols]
        amp = amp_ref[:, cols]
        decay = jnp.exp(-float(rows * blocks) * rate)
        running = jnp.zeros((modes, LANES), F32)
        entering = jnp.zeros((modes, LANES), F32)
        for chunk in range(chunks_ref.shape[0]):
            entering = jnp.where(own == chunk, running, entering)
            running = decay * running + chunks_ref[chunk, :, cols]
        steps = [jnp.exp(-8.0 * j * rate) for j in range(tiles)]
        first = tile_rows() + 1.0
        aheads = [jnp.exp(-rate[m : m + 1] * first) for m in range(modes)]
        state = entering
        for i in range(blocks):
            full = (before_ref[i, :, cols] + state) * amp
            if i < blocks - 1:
                state = state * jnp.exp(-float(rows) * rate)
            parts = []
            for j in range(tiles):
                part = base_ref[i, 8 * j : 8 * j + 8, cols]
                scaled = full * steps[j]
                for m in range(modes):
                    part = part + scaled[m : m + 1] * aheads[m]
                parts.append(part)
            gate = inputs_ref[i % cores, i // cores, 2, :, source].astype(F32)
            gated_ref[i, :, cols] = (gate * jnp.concatenate(parts, axis=0)).astype(BF16)
        return carry

    lax.fori_loop(0, width // LANES, slab, 0)


def project_kernel(gated_ref, near_ref, far_ref, out_ref):
    cores, shared, rows, half = gated_ref.shape
    gated = [gated_ref[core].reshape(shared * rows, half) for core in range(cores)]
    for j in range(out_ref.shape[0]):
        total = 0.0
        for core in range(cores):
            depth = slice(core * half, (core + 1) * half)
            weight = jnp.concatenate([near_ref[j, :, depth], far_ref[j, :, depth]], axis=0)
            total = total + lax.dot_general(
                gated[core], weight, (((1,), (1,)), ((), ())), preferred_element_type=F32
            )
        out_ref[j] = total.astype(BF16).reshape(out_ref.shape[1:])


def sum_kernel(parts_ref, out_ref):
    groups, low, cores, rows, width = parts_ref.shape
    own_high = lax.axis_index("xh")
    unit = width // 2
    for x_low in range(low):
        totals = []
        for core in range(cores):
            total = parts_ref[0, x_low, core].astype(F32)
            for j in range(1, groups):
                total = total + parts_ref[j, x_low, core].astype(F32)
            totals.append(total)
        near = [total[:, :unit] for total in totals]
        far = [total[:, unit:] for total in totals]
        near, far = jnp.concatenate(near, axis=1), jnp.concatenate(far, axis=1)
        for high in range(2):
            place = (high * low + x_low) * (cores * unit)
            columns = jnp.where(own_high == high, near, far)
            out_ref[:, place : place + cores * unit] = columns.astype(BF16)


def exchange(x, axes):
    return lax.all_to_all(x, axes, 0, 0, tiled=True)


def body(gate_input, key_input, value_input, decay_rate, residue, skip_gain, out_weight):
    rows, width = key_input.shape
    modes = decay_rate.shape[0]
    z_size, high_size, low_size, cores = (lax.axis_size(a) for a in SEQ)
    y_size = lax.axis_size("chan")
    out_cols = out_weight.shape[1]
    chunks = z_size * high_size
    blocks = low_size * cores
    half = width // cores
    own_weight = jnp.broadcast_to(out_weight.T[None], (z_size, out_cols, width))
    near = exchange(own_weight, "z")
    inputs = jnp.stack([key_input, value_input, gate_input])
    inputs = lax.all_gather(lax.all_gather(inputs, "xl"), "core")
    base, before, state, amplitude, rate = pl.pallas_call(
        chunk_kernel,
        out_shape=(
            jax.ShapeDtypeStruct((blocks, rows, half), F32),
            jax.ShapeDtypeStruct((blocks, modes, half), F32),
            jax.ShapeDtypeStruct((chunks, modes, half), F32),
            jax.ShapeDtypeStruct((modes, half), F32),
            jax.ShapeDtypeStruct((modes, half), F32),
        ),
        in_specs=[VMEM] * 4,
        out_specs=(VMEM,) * 5,
        scratch_shapes=[
            pltpu.VMEM((blocks, rows, LANES), F32),
            pltpu.VMEM((blocks, modes, LANES), F32),
        ],
        compiler_params=PARAMS,
        name="chunk",
    )(inputs, decay_rate, residue, skip_gain[None, :])
    state, near = lax.optimization_barrier((state, near))
    far = lax.ppermute(near, "xh", [(0, 1), (1, 0)])
    states = exchange(state, ("z", "xh"))
    gated = pl.pallas_call(
        gate_kernel,
        out_shape=jax.ShapeDtypeStruct((blocks, rows, half), BF16),
        in_specs=[VMEM] * 6,
        out_specs=VMEM,
        compiler_params=PARAMS,
        name="gate",
    )(states, before, rate, amplitude, base, inputs)
    gated, far = lax.optimization_barrier((gated, far))
    gated = lax.all_gather(gated, "core")
    piece = (rows, high_size * out_cols)
    parts = pl.pallas_call(
        project_kernel,
        out_shape=jax.ShapeDtypeStruct((y_size, blocks) + piece, BF16),
        in_specs=[VMEM] * 3,
        out_specs=VMEM,
        compiler_params=PARAMS,
        name="project",
    )(gated, near, far)
    parts = exchange(parts.reshape((y_size * blocks,) + piece), ("chan", "xl", "core"))
    return pl.pallas_call(
        sum_kernel,
        out_shape=jax.ShapeDtypeStruct((rows, width), BF16),
        in_specs=[VMEM],
        out_specs=VMEM,
        compiler_params=PARAMS,
        name="sum_parts",
    )(parts.reshape((y_size, low_size, cores) + piece))


def solution(mesh):
    finer = Mesh(mesh.devices.reshape(8, 2, 2, 2, 8), SEQ + ("chan",))
    return jax.shard_map(
        body,
        mesh=finer,
        in_specs=(
            P(SEQ, "chan"),
            P(SEQ, "chan"),
            P(SEQ, "chan"),
            P(None, "chan"),
            P(None, "chan"),
            P("chan"),
            P("chan", SEQ),
        ),
        out_specs=P(SEQ, "chan"),
        check_vma=False,
    )
```

```python
import jax
import jax.numpy as jnp
from jax import lax
from jax.experimental import pallas as pl
from jax.experimental.pallas import tpu as pltpu
from jax.sharding import Mesh
from jax.sharding import PartitionSpec as P

F32 = jnp.float32
BF16 = jnp.bfloat16
SEQ = ("z", "xh", "xl", "core")
LANES = 128
VMEM = pl.BlockSpec(memory_space=pltpu.VMEM)
PARAMS = pltpu.CompilerParams(vmem_limit_bytes=48 * 1024 * 1024)


def tile_rows():
    return lax.broadcasted_iota(jnp.int32, (8, LANES), 0).astype(F32)


def chunk_kernel(
    inputs_ref, rate_ref, residue_ref, skip_ref,
    base_ref, before_ref, send_ref, amp_ref, copy_ref, signal_ref, state_ref,
):
    blocks, rows, width = base_ref.shape
    modes = rate_ref.shape[0]
    tiles = rows // 8
    cores = inputs_ref.shape[0]
    first_col = lax.axis_index("core") * width

    def slab(index, carry):
        cols = pl.ds(pl.multiple_of(index * LANES, LANES), LANES)
        source = pl.ds(pl.multiple_of(first_col + index * LANES, LANES), LANES)
        for i in range(blocks):
            key = inputs_ref[i % cores, i // cores, 0, :, source].astype(F32)
            signal_ref[i] = key * inputs_ref[i % cores, i // cores, 1, :, source].astype(F32)
        rate = rate_ref[:, source]
        amp = residue_ref[:, source] * jnp.sqrt(1.0 - jnp.exp(-2.0 * rate))
        amp_ref[:, cols] = amp
        copy_ref[:, cols] = rate
        steps = [jnp.exp(-8.0 * j * rate) for j in range(tiles)]
        scaled = [amp * step for step in steps]
        first = tile_rows()
        taps = [jnp.zeros((8, LANES), F32) for _ in range(tiles)]
        for m in range(modes):
            ahead = jnp.exp(-rate[m : m + 1] * first)
            behind = jnp.exp(-rate[m : m + 1] * (7.0 - first))
            held = [jnp.zeros((8, LANES), F32) for _ in range(blocks)]
            for j in range(tiles):
                taps[j] = taps[j] + scaled[j][m : m + 1] * ahead
                step = steps[tiles - 1 - j][m : m + 1]
                for i in range(blocks):
                    held[i] = held[i] + step * signal_ref[i, 8 * j : 8 * j + 8]
            for i in range(blocks):
                state_ref[i, m : m + 1] = jnp.sum(held[i] * behind, axis=0, keepdims=True)
        decay = jnp.exp(-float(rows) * rate)
        running = jnp.zeros((modes, LANES), F32)
        for i in range(blocks):
            before_ref[i, :, cols] = running
            running = decay * running + state_ref[i]
        send_ref[:, cols] = running
        row_ids = lax.broadcasted_iota(jnp.int32, (rows, LANES), 0)
        skip = skip_ref[0:1, source]

        def block(i, inner):
            signal = signal_ref[i]
            totals = [skip * signal[8 * j : 8 * j + 8] for j in range(tiles)]
            for lag in range(8):
                moved = signal
                if lag:
                    moved = jnp.where(row_ids >= lag, pltpu.roll(signal, lag, 0), 0.0)
                for j in range(tiles):
                    tap = taps[j][lag : lag + 1]
                    for k in range(j, tiles):
                        totals[k] = totals[k] + tap * moved[8 * (k - j) : 8 * (k - j) + 8]
            for j in range(tiles):
                base_ref[i, 8 * j : 8 * j + 8, cols] = totals[j]
            return inner

        return lax.fori_loop(0, blocks, block, carry)

    lax.fori_loop(0, width // LANES, slab, 0)


def total_kernel(length, states_ref, rate_ref, total_ref):
    decay = jnp.exp(-float(length) * rate_ref[...])
    total = states_ref[0]
    for i in range(1, states_ref.shape[0]):
        total = decay * total + states_ref[i]
    for copy in range(total_ref.shape[0]):
        total_ref[copy] = total


def gate_kernel(
    totals_ref, states_ref, before_ref, rate_ref, amp_ref, base_ref, inputs_ref, gated_ref
):
    blocks, rows, width = base_ref.shape
    modes = rate_ref.shape[0]
    tiles = rows // 8
    cores = inputs_ref.shape[0]
    own_z = lax.axis_index("z")
    own_high = lax.axis_index("xh")
    first_col = lax.axis_index("core") * width
    highs = states_ref.shape[0]

    def slab(index, carry):
        cols = pl.ds(pl.multiple_of(index * LANES, LANES), LANES)
        source = pl.ds(pl.multiple_of(first_col + index * LANES, LANES), LANES)
        rate = rate_ref[:, cols]
        amp = amp_ref[:, cols]
        decay = jnp.exp(-float(rows * blocks * highs) * rate)
        running = jnp.zeros((modes, LANES), F32)
        entering = jnp.zeros((modes, LANES), F32)
        for z in range(totals_ref.shape[0]):
            entering = jnp.where(own_z == z, running, entering)
            running = decay * running + totals_ref[z, :, cols]
        decay = jnp.exp(-float(rows * blocks) * rate)
        running = entering
        for high in range(1, highs):
            running = decay * running + states_ref[high - 1, :, cols]
            entering = jnp.where(own_high == high, running, entering)
        steps = [jnp.exp(-8.0 * j * rate) for j in range(tiles)]
        first = tile_rows() + 1.0
        aheads = [jnp.exp(-rate[m : m + 1] * first) for m in range(modes)]
        state = entering
        for i in range(blocks):
            full = (before_ref[i, :, cols] + state) * amp
            if i < blocks - 1:
                state = state * jnp.exp(-float(rows) * rate)
            parts = []
            for j in range(tiles):
                part = base_ref[i, 8 * j : 8 * j + 8, cols]
                scaled = full * steps[j]
                for m in range(modes):
                    part = part + scaled[m : m + 1] * aheads[m]
                parts.append(part)
            gate = inputs_ref[i % cores, i // cores, 2, :, source].astype(F32)
            gated_ref[i, :, cols] = (gate * jnp.concatenate(parts, axis=0)).astype(BF16)
        return carry

    lax.fori_loop(0, width // LANES, slab, 0)


def project_kernel(gated_ref, near_ref, far_ref, out_ref):
    cores, shared, rows, half = gated_ref.shape
    gated = [gated_ref[core].reshape(shared * rows, half) for core in range(cores)]
    for j in range(out_ref.shape[0]):
        total = 0.0
        for core in range(cores):
            depth = slice(core * half, (core + 1) * half)
            weight = jnp.concatenate([near_ref[j, :, depth], far_ref[j, :, depth]], axis=0)
            total = total + lax.dot_general(
                gated[core], weight, (((1,), (1,)), ((), ())), preferred_element_type=F32
            )
        out_ref[j] = total.astype(BF16).reshape(out_ref.shape[1:])


def sum_kernel(parts_ref, out_ref):
    groups, low, cores, rows, width = parts_ref.shape
    own_high = lax.axis_index("xh")
    unit = width // 2
    for x_low in range(low):
        totals = []
        for core in range(cores):
            total = parts_ref[0, x_low, core].astype(F32)
            for j in range(1, groups):
                total = total + parts_ref[j, x_low, core].astype(F32)
            totals.append(total)
        near = [total[:, :unit] for total in totals]
        far = [total[:, unit:] for total in totals]
        near, far = jnp.concatenate(near, axis=1), jnp.concatenate(far, axis=1)
        for high in range(2):
            place = (high * low + x_low) * (cores * unit)
            columns = jnp.where(own_high == high, near, far)
            out_ref[:, place : place + cores * unit] = columns.astype(BF16)


def exchange(x, axes):
    return lax.all_to_all(x, axes, 0, 0, tiled=True)


def body(gate_input, key_input, value_input, decay_rate, residue, skip_gain, out_weight):
    rows, width = key_input.shape
    modes = decay_rate.shape[0]
    z_size, high_size, low_size, cores = (lax.axis_size(a) for a in SEQ)
    y_size = lax.axis_size("chan")
    out_cols = out_weight.shape[1]
    blocks = low_size * cores
    half = width // cores
    own_weight = jnp.broadcast_to(out_weight.T[None], (z_size, out_cols, width))
    near = exchange(own_weight, "z")
    inputs = jnp.stack([key_input, value_input, gate_input])
    inputs = lax.all_gather(lax.all_gather(inputs, "xl"), "core")
    base, before, state, amplitude, rate = pl.pallas_call(
        chunk_kernel,
        out_shape=(
            jax.ShapeDtypeStruct((blocks, rows, half), F32),
            jax.ShapeDtypeStruct((blocks, modes, half), F32),
            jax.ShapeDtypeStruct((modes, half), F32),
            jax.ShapeDtypeStruct((modes, half), F32),
            jax.ShapeDtypeStruct((modes, half), F32),
        ),
        in_specs=[VMEM] * 4,
        out_specs=(VMEM,) * 5,
        scratch_shapes=[
            pltpu.VMEM((blocks, rows, LANES), F32),
            pltpu.VMEM((blocks, modes, LANES), F32),
        ],
        compiler_params=PARAMS,
        name="chunk",
    )(inputs, decay_rate, residue, skip_gain[None, :])
    states = lax.all_gather(state, "xh")
    total = pl.pallas_call(
        lambda *refs: total_kernel(rows * blocks, *refs),
        out_shape=jax.ShapeDtypeStruct((z_size, modes, half), F32),
        in_specs=[VMEM] * 2,
        out_specs=VMEM,
        compiler_params=PARAMS,
        name="total",
    )(states, rate)
    total, near = lax.optimization_barrier((total, near))
    far = lax.ppermute(near, "xh", [(0, 1), (1, 0)])
    totals = exchange(total, "z")
    gated = pl.pallas_call(
        gate_kernel,
        out_shape=jax.ShapeDtypeStruct((blocks, rows, half), BF16),
        in_specs=[VMEM] * 7,
        out_specs=VMEM,
        compiler_params=PARAMS,
        name="gate",
    )(totals, states, before, rate, amplitude, base, inputs)
    gated, far = lax.optimization_barrier((gated, far))
    gated = lax.all_gather(gated, "core")
    piece = (rows, high_size * out_cols)
    parts = pl.pallas_call(
        project_kernel,
        out_shape=jax.ShapeDtypeStruct((y_size, blocks) + piece, BF16),
        in_specs=[VMEM] * 3,
        out_specs=VMEM,
        compiler_params=PARAMS,
        name="project",
    )(gated, near, far)
    parts = exchange(parts.reshape((y_size * blocks,) + piece), ("chan", "xl", "core"))
    return pl.pallas_call(
        sum_kernel,
        out_shape=jax.ShapeDtypeStruct((rows, width), BF16),
        in_specs=[VMEM],
        out_specs=VMEM,
        compiler_params=PARAMS,
        name="sum_parts",
    )(parts.reshape((y_size, low_size, cores) + piece))


def solution(mesh):
    finer = Mesh(mesh.devices.reshape(8, 2, 2, 2, 8), SEQ + ("chan",))
    return jax.shard_map(
        body,
        mesh=finer,
        in_specs=(
            P(SEQ, "chan"),
            P(SEQ, "chan"),
            P(SEQ, "chan"),
            P(None, "chan"),
            P(None, "chan"),
            P("chan"),
            P("chan", SEQ),
        ),
        out_specs=P(SEQ, "chan"),
        check_vma=False,
    )
```

```python
import jax
import jax.numpy as jnp
from jax import lax
from jax.experimental import pallas as pl
from jax.experimental.pallas import tpu as pltpu
from jax.sharding import Mesh
from jax.sharding import PartitionSpec as P

F32 = jnp.float32
BF16 = jnp.bfloat16
SEQ = ("z", "xh", "xl", "core")
LANES = 128
VMEM = pl.BlockSpec(memory_space=pltpu.VMEM)
PARAMS = pltpu.CompilerParams(vmem_limit_bytes=48 * 1024 * 1024)


def tile_rows():
    return lax.broadcasted_iota(jnp.int32, (8, LANES), 0).astype(F32)


def chunk_kernel(
    inputs_ref, rate_ref, residue_ref, skip_ref,
    base_ref, before_ref, send_ref, amp_ref, copy_ref, signal_ref, state_ref,
):
    blocks, rows, width = base_ref.shape
    modes = rate_ref.shape[0]
    tiles = rows // 8
    cores = inputs_ref.shape[0]
    first_col = lax.axis_index("core") * width

    def slab(index, carry):
        cols = pl.ds(pl.multiple_of(index * LANES, LANES), LANES)
        source = pl.ds(pl.multiple_of(first_col + index * LANES, LANES), LANES)
        for i in range(blocks):
            key = inputs_ref[i % cores, i // cores, 0, :, source].astype(F32)
            signal_ref[i] = key * inputs_ref[i % cores, i // cores, 1, :, source].astype(F32)
        rate = rate_ref[:, source]
        amp = residue_ref[:, source] * jnp.sqrt(1.0 - jnp.exp(-2.0 * rate))
        amp_ref[:, cols] = amp
        copy_ref[:, cols] = rate
        steps = [jnp.exp(-8.0 * j * rate) for j in range(tiles)]
        scaled = [amp * step for step in steps]
        first = tile_rows()
        taps = [jnp.zeros((8, LANES), F32) for _ in range(tiles)]
        for m in range(modes):
            ahead = jnp.exp(-rate[m : m + 1] * first)
            behind = jnp.exp(-rate[m : m + 1] * (7.0 - first))
            held = [jnp.zeros((8, LANES), F32) for _ in range(blocks)]
            for j in range(tiles):
                taps[j] = taps[j] + scaled[j][m : m + 1] * ahead
                step = steps[tiles - 1 - j][m : m + 1]
                for i in range(blocks):
                    held[i] = held[i] + step * signal_ref[i, 8 * j : 8 * j + 8]
            for i in range(blocks):
                state_ref[i, m : m + 1] = jnp.sum(held[i] * behind, axis=0, keepdims=True)
        decay = jnp.exp(-float(rows) * rate)
        running = jnp.zeros((modes, LANES), F32)
        for i in range(blocks):
            before_ref[i, :, cols] = running
            running = decay * running + state_ref[i]
        send_ref[:, cols] = running
        row_ids = lax.broadcasted_iota(jnp.int32, (rows, LANES), 0)
        skip = skip_ref[0:1, source]

        def block(i, inner):
            signal = signal_ref[i]
            totals = [skip * signal[8 * j : 8 * j + 8] for j in range(tiles)]
            for lag in range(8):
                moved = signal
                if lag:
                    moved = jnp.where(row_ids >= lag, pltpu.roll(signal, lag, 0), 0.0)
                for j in range(tiles):
                    tap = taps[j][lag : lag + 1]
                    for k in range(j, tiles):
                        totals[k] = totals[k] + tap * moved[8 * (k - j) : 8 * (k - j) + 8]
            for j in range(tiles):
                base_ref[i, 8 * j : 8 * j + 8, cols] = totals[j]
            return inner

        return lax.fori_loop(0, blocks, block, carry)

    lax.fori_loop(0, width // LANES, slab, 0)


def total_kernel(length, states_ref, rate_ref, total_ref):
    decay = jnp.exp(-float(length) * rate_ref[...])
    total = states_ref[0]
    for i in range(1, states_ref.shape[0]):
        total = decay * total + states_ref[i]
    for copy in range(total_ref.shape[0]):
        total_ref[copy] = total


def gate_kernel(
    totals_ref, states_ref, before_ref, rate_ref, amp_ref, base_ref, inputs_ref, gated_ref
):
    blocks, rows, width = base_ref.shape
    modes = rate_ref.shape[0]
    tiles = rows // 8
    cores = inputs_ref.shape[0]
    own_z = lax.axis_index("z")
    own_high = lax.axis_index("xh")
    first_col = lax.axis_index("core") * width
    highs = states_ref.shape[0]

    def slab(index, carry):
        cols = pl.ds(pl.multiple_of(index * LANES, LANES), LANES)
        source = pl.ds(pl.multiple_of(first_col + index * LANES, LANES), LANES)
        rate = rate_ref[:, cols]
        amp = amp_ref[:, cols]
        decay = jnp.exp(-float(rows * blocks * highs) * rate)
        running = jnp.zeros((modes, LANES), F32)
        entering = jnp.zeros((modes, LANES), F32)
        for z in range(totals_ref.shape[0]):
            entering = jnp.where(own_z == z, running, entering)
            running = decay * running + totals_ref[z, :, cols]
        decay = jnp.exp(-float(rows * blocks) * rate)
        running = entering
        for high in range(1, highs):
            running = decay * running + states_ref[high - 1, :, cols]
            entering = jnp.where(own_high == high, running, entering)
        steps = [jnp.exp(-8.0 * j * rate) for j in range(tiles)]
        first = tile_rows() + 1.0
        aheads = [jnp.exp(-rate[m : m + 1] * first) for m in range(modes)]
        state = entering
        for i in range(blocks):
            full = (before_ref[i, :, cols] + state) * amp
            if i < blocks - 1:
                state = state * jnp.exp(-float(rows) * rate)
            parts = []
            for j in range(tiles):
                part = base_ref[i, 8 * j : 8 * j + 8, cols]
                scaled = full * steps[j]
                for m in range(modes):
                    part = part + scaled[m : m + 1] * aheads[m]
                parts.append(part)
            gate = inputs_ref[i % cores, i // cores, 2, :, source].astype(F32)
            gated_ref[i, :, cols] = (gate * jnp.concatenate(parts, axis=0)).astype(BF16)
        return carry

    lax.fori_loop(0, width // LANES, slab, 0)


def project_kernel(gated_ref, near_ref, far_ref, out_ref):
    cores, shared, rows, half = gated_ref.shape
    gated = [gated_ref[core].reshape(shared * rows, half) for core in range(cores)]
    for j in range(out_ref.shape[0]):
        total = 0.0
        for core in range(cores):
            depth = slice(core * half, (core + 1) * half)
            weight = jnp.concatenate([near_ref[j, :, depth], far_ref[j, :, depth]], axis=0)
            total = total + lax.dot_general(
                gated[core], weight, (((1,), (1,)), ((), ())), preferred_element_type=F32
            )
        out_ref[j] = total.astype(BF16).reshape(out_ref.shape[1:])


def sum_kernel(parts_ref, out_ref):
    groups, low, cores, rows, width = parts_ref.shape
    own_high = lax.axis_index("xh")
    unit = width // 2
    for x_low in range(low):
        totals = []
        for core in range(cores):
            total = parts_ref[0, x_low, core].astype(F32)
            for j in range(1, groups):
                total = total + parts_ref[j, x_low, core].astype(F32)
            totals.append(total)
        near = [total[:, :unit] for total in totals]
        far = [total[:, unit:] for total in totals]
        near, far = jnp.concatenate(near, axis=1), jnp.concatenate(far, axis=1)
        for high in range(2):
            place = (high * low + x_low) * (cores * unit)
            columns = jnp.where(own_high == high, near, far)
            out_ref[:, place : place + cores * unit] = columns.astype(BF16)


def exchange(x, axes):
    return lax.all_to_all(x, axes, 0, 0, tiled=True)


def body(gate_input, key_input, value_input, decay_rate, residue, skip_gain, out_weight):
    rows, width = key_input.shape
    modes = decay_rate.shape[0]
    z_size, high_size, low_size, cores = (lax.axis_size(a) for a in SEQ)
    y_size = lax.axis_size("chan")
    out_cols = out_weight.shape[1]
    blocks = low_size * cores
    half = width // cores
    own_weight = jnp.broadcast_to(out_weight.T[None], (z_size, out_cols, width))
    near = exchange(own_weight, "z")
    inputs = jnp.stack([key_input, value_input, gate_input])
    inputs = lax.all_gather(lax.all_gather(inputs, "xl"), "core")
    base, before, state, amplitude, rate = pl.pallas_call(
        chunk_kernel,
        out_shape=(
            jax.ShapeDtypeStruct((blocks, rows, half), F32),
            jax.ShapeDtypeStruct((blocks, modes, half), F32),
            jax.ShapeDtypeStruct((modes, half), F32),
            jax.ShapeDtypeStruct((modes, half), F32),
            jax.ShapeDtypeStruct((modes, half), F32),
        ),
        in_specs=[VMEM] * 4,
        out_specs=(VMEM,) * 5,
        scratch_shapes=[
            pltpu.VMEM((blocks, rows, LANES), F32),
            pltpu.VMEM((blocks, modes, LANES), F32),
        ],
        compiler_params=PARAMS,
        name="chunk",
    )(inputs, decay_rate, residue, skip_gain[None, :])
    states = lax.all_gather(state, "xh")
    total = pl.pallas_call(
        lambda *refs: total_kernel(rows * blocks, *refs),
        out_shape=jax.ShapeDtypeStruct((z_size, modes, half), F32),
        in_specs=[VMEM] * 2,
        out_specs=VMEM,
        compiler_params=PARAMS,
        name="total",
    )(states, rate)
    total, near = lax.optimization_barrier((total, near))
    far = lax.ppermute(near, "xh", [(0, 1), (1, 0)])
    totals = exchange(total, "z")
    gated = pl.pallas_call(
        gate_kernel,
        out_shape=jax.ShapeDtypeStruct((blocks, rows, half), BF16),
        in_specs=[VMEM] * 7,
        out_specs=VMEM,
        compiler_params=PARAMS,
        name="gate",
    )(totals, states, before, rate, amplitude, base, inputs)
    gated = lax.all_gather(gated, "core")
    piece = (rows, high_size * out_cols)
    parts = pl.pallas_call(
        project_kernel,
        out_shape=jax.ShapeDtypeStruct((y_size, blocks) + piece, BF16),
        in_specs=[VMEM] * 3,
        out_specs=VMEM,
        compiler_params=PARAMS,
        name="project",
    )(gated, near, far)
    parts = exchange(parts.reshape((y_size * blocks,) + piece), ("chan", "xl", "core"))
    return pl.pallas_call(
        sum_kernel,
        out_shape=jax.ShapeDtypeStruct((rows, width), BF16),
        in_specs=[VMEM],
        out_specs=VMEM,
        compiler_params=PARAMS,
        name="sum_parts",
    )(parts.reshape((y_size, low_size, cores) + piece))


def solution(mesh):
    finer = Mesh(mesh.devices.reshape(8, 2, 2, 2, 8), SEQ + ("chan",))
    return jax.shard_map(
        body,
        mesh=finer,
        in_specs=(
            P(SEQ, "chan"),
            P(SEQ, "chan"),
            P(SEQ, "chan"),
            P(None, "chan"),
            P(None, "chan"),
            P("chan"),
            P("chan", SEQ),
        ),
        out_specs=P(SEQ, "chan"),
        check_vma=False,
    )
```

```python
import jax
import jax.numpy as jnp
from jax import lax
from jax.experimental import pallas as pl
from jax.experimental.pallas import tpu as pltpu
from jax.sharding import Mesh
from jax.sharding import PartitionSpec as P

F32 = jnp.float32
BF16 = jnp.bfloat16
SEQ = ("z", "xh", "xl", "core")
LANES = 128
VMEM = pl.BlockSpec(memory_space=pltpu.VMEM)
PARAMS = pltpu.CompilerParams(vmem_limit_bytes=48 * 1024 * 1024)


def tile_rows():
    return lax.broadcasted_iota(jnp.int32, (8, LANES), 0).astype(F32)


def chunk_kernel(
    inputs_ref, rate_ref, residue_ref, skip_ref,
    base_ref, before_ref, send_ref, amp_ref, copy_ref, signal_ref, state_ref,
):
    blocks, rows, width = base_ref.shape
    modes = rate_ref.shape[0]
    tiles = rows // 8
    cores = inputs_ref.shape[0]
    first_col = lax.axis_index("core") * width

    def slab(index, carry):
        cols = pl.ds(pl.multiple_of(index * LANES, LANES), LANES)
        source = pl.ds(pl.multiple_of(first_col + index * LANES, LANES), LANES)
        for i in range(blocks):
            key = inputs_ref[i % cores, i // cores, 0, :, source].astype(F32)
            signal_ref[i] = key * inputs_ref[i % cores, i // cores, 1, :, source].astype(F32)
        rate = rate_ref[:, source]
        amp = residue_ref[:, source] * jnp.sqrt(1.0 - jnp.exp(-2.0 * rate))
        amp_ref[:, cols] = amp
        copy_ref[:, cols] = rate
        steps = [jnp.exp(-8.0 * j * rate) for j in range(tiles)]
        scaled = [amp * step for step in steps]
        first = tile_rows()
        taps = [jnp.zeros((8, LANES), F32) for _ in range(tiles)]
        for m in range(modes):
            ahead = jnp.exp(-rate[m : m + 1] * first)
            behind = jnp.exp(-rate[m : m + 1] * (7.0 - first))
            held = [jnp.zeros((8, LANES), F32) for _ in range(blocks)]
            for j in range(tiles):
                taps[j] = taps[j] + scaled[j][m : m + 1] * ahead
                step = steps[tiles - 1 - j][m : m + 1]
                for i in range(blocks):
                    held[i] = held[i] + step * signal_ref[i, 8 * j : 8 * j + 8]
            for i in range(blocks):
                state_ref[i, m : m + 1] = jnp.sum(held[i] * behind, axis=0, keepdims=True)
        decay = jnp.exp(-float(rows) * rate)
        running = jnp.zeros((modes, LANES), F32)
        for i in range(blocks):
            before_ref[i, :, cols] = running
            running = decay * running + state_ref[i]
        send_ref[:, cols] = running
        row_ids = lax.broadcasted_iota(jnp.int32, (rows, LANES), 0)
        skip = skip_ref[0:1, source]

        def block(i, inner):
            signal = signal_ref[i]
            totals = [skip * signal[8 * j : 8 * j + 8] for j in range(tiles)]
            for lag in range(8):
                moved = signal
                if lag:
                    moved = jnp.where(row_ids >= lag, pltpu.roll(signal, lag, 0), 0.0)
                for j in range(tiles):
                    tap = taps[j][lag : lag + 1]
                    for k in range(j, tiles):
                        totals[k] = totals[k] + tap * moved[8 * (k - j) : 8 * (k - j) + 8]
            for j in range(tiles):
                base_ref[i, 8 * j : 8 * j + 8, cols] = totals[j]
            return inner

        return lax.fori_loop(0, blocks, block, carry)

    lax.fori_loop(0, width // LANES, slab, 0)


def total_kernel(length, states_ref, rate_ref, total_ref):
    decay = jnp.exp(-float(length) * rate_ref[...])
    total = states_ref[0]
    for i in range(1, states_ref.shape[0]):
        total = decay * total + states_ref[i]
    for copy in range(total_ref.shape[0]):
        total_ref[copy] = total


def gate_kernel(
    totals_ref, states_ref, before_ref, rate_ref, amp_ref, base_ref, inputs_ref, gated_ref
):
    blocks, rows, width = base_ref.shape
    modes = rate_ref.shape[0]
    tiles = rows // 8
    cores = inputs_ref.shape[0]
    own_z = lax.axis_index("z")
    own_high = lax.axis_index("xh")
    first_col = lax.axis_index("core") * width
    highs = states_ref.shape[0]

    def slab(index, carry):
        cols = pl.ds(pl.multiple_of(index * LANES, LANES), LANES)
        source = pl.ds(pl.multiple_of(first_col + index * LANES, LANES), LANES)
        rate = rate_ref[:, cols]
        amp = amp_ref[:, cols]
        decay = jnp.exp(-float(rows * blocks * highs) * rate)
        running = jnp.zeros((modes, LANES), F32)
        entering = jnp.zeros((modes, LANES), F32)
        for z in range(totals_ref.shape[0]):
            entering = jnp.where(own_z == z, running, entering)
            running = decay * running + totals_ref[z, :, cols]
        decay = jnp.exp(-float(rows * blocks) * rate)
        running = entering
        for high in range(1, highs):
            running = decay * running + states_ref[high - 1, :, cols]
            entering = jnp.where(own_high == high, running, entering)
        steps = [jnp.exp(-8.0 * j * rate) for j in range(tiles)]
        first = tile_rows() + 1.0
        aheads = [jnp.exp(-rate[m : m + 1] * first) for m in range(modes)]
        state = entering
        for i in range(blocks):
            full = (before_ref[i, :, cols] + state) * amp
            if i < blocks - 1:
                state = state * jnp.exp(-float(rows) * rate)
            parts = []
            for j in range(tiles):
                part = base_ref[i, 8 * j : 8 * j + 8, cols]
                scaled = full * steps[j]
                for m in range(modes):
                    part = part + scaled[m : m + 1] * aheads[m]
                parts.append(part)
            gate = inputs_ref[i % cores, i // cores, 2, :, source].astype(F32)
            gated_ref[i, :, cols] = (gate * jnp.concatenate(parts, axis=0)).astype(BF16)
        return carry

    lax.fori_loop(0, width // LANES, slab, 0)


def project_kernel(gated_ref, near_ref, far_ref, out_ref):
    cores, shared, rows, half = gated_ref.shape
    gated = [gated_ref[core].reshape(shared * rows, half) for core in range(cores)]
    for j in range(out_ref.shape[1]):
        total = 0.0
        for core in range(cores):
            depth = slice(core * half, (core + 1) * half)
            weight = jnp.concatenate([near_ref[j, :, depth], far_ref[j, :, depth]], axis=0)
            total = total + lax.dot_general(
                gated[core], weight, (((1,), (1,)), ((), ())), preferred_element_type=F32
            )
        out_ref[:, j] = total.astype(BF16).reshape(shared, rows, -1)


def sum_kernel(parts_ref, out_ref):
    low, cores, groups, rows, width = parts_ref.shape
    own_high = lax.axis_index("xh")
    unit = width // 2
    for x_low in range(low):
        totals = []
        for core in range(cores):
            total = parts_ref[x_low, core, 0].astype(F32)
            for j in range(1, groups):
                total = total + parts_ref[x_low, core, j].astype(F32)
            totals.append(total)
        near = [total[:, :unit] for total in totals]
        far = [total[:, unit:] for total in totals]
        near, far = jnp.concatenate(near, axis=1), jnp.concatenate(far, axis=1)
        for high in range(2):
            place = (high * low + x_low) * (cores * unit)
            columns = jnp.where(own_high == high, near, far)
            out_ref[:, place : place + cores * unit] = columns.astype(BF16)


def exchange(x, axes):
    return lax.all_to_all(x, axes, 0, 0, tiled=True)


def body(gate_input, key_input, value_input, decay_rate, residue, skip_gain, out_weight):
    rows, width = key_input.shape
    modes = decay_rate.shape[0]
    z_size, high_size, low_size, cores = (lax.axis_size(a) for a in SEQ)
    y_size = lax.axis_size("chan")
    out_cols = out_weight.shape[1]
    blocks = low_size * cores
    half = width // cores
    own_weight = jnp.broadcast_to(out_weight.T[None], (z_size, out_cols, width))
    near = exchange(own_weight, "z")
    inputs = jnp.stack([key_input, value_input, gate_input])
    inputs = lax.all_gather(lax.all_gather(inputs, "xl"), "core")
    base, before, state, amplitude, rate = pl.pallas_call(
        chunk_kernel,
        out_shape=(
            jax.ShapeDtypeStruct((blocks, rows, half), F32),
            jax.ShapeDtypeStruct((blocks, modes, half), F32),
            jax.ShapeDtypeStruct((modes, half), F32),
            jax.ShapeDtypeStruct((modes, half), F32),
            jax.ShapeDtypeStruct((modes, half), F32),
        ),
        in_specs=[VMEM] * 4,
        out_specs=(VMEM,) * 5,
        scratch_shapes=[
            pltpu.VMEM((blocks, rows, LANES), F32),
            pltpu.VMEM((blocks, modes, LANES), F32),
        ],
        compiler_params=PARAMS,
        name="chunk",
    )(inputs, decay_rate, residue, skip_gain[None, :])
    states = lax.all_gather(state, "xh")
    total = pl.pallas_call(
        lambda *refs: total_kernel(rows * blocks, *refs),
        out_shape=jax.ShapeDtypeStruct((z_size, modes, half), F32),
        in_specs=[VMEM] * 2,
        out_specs=VMEM,
        compiler_params=PARAMS,
        name="total",
    )(states, rate)
    total, near = lax.optimization_barrier((total, near))
    far = lax.ppermute(near, "xh", [(0, 1), (1, 0)])
    totals = exchange(total, "z")
    gated = pl.pallas_call(
        gate_kernel,
        out_shape=jax.ShapeDtypeStruct((blocks, rows, half), BF16),
        in_specs=[VMEM] * 7,
        out_specs=VMEM,
        compiler_params=PARAMS,
        name="gate",
    )(totals, states, before, rate, amplitude, base, inputs)
    gated = lax.all_gather(gated, "core")
    piece = (rows, high_size * out_cols)
    parts = pl.pallas_call(
        project_kernel,
        out_shape=jax.ShapeDtypeStruct((blocks, y_size) + piece, BF16),
        in_specs=[VMEM] * 3,
        out_specs=VMEM,
        compiler_params=PARAMS,
        name="project",
    )(gated, near, far)
    parts = exchange(parts.reshape((y_size * blocks,) + piece), ("xl", "core", "chan"))
    return pl.pallas_call(
        sum_kernel,
        out_shape=jax.ShapeDtypeStruct((rows, width), BF16),
        in_specs=[VMEM],
        out_specs=VMEM,
        compiler_params=PARAMS,
        name="sum_parts",
    )(parts.reshape((low_size, cores, y_size) + piece))


def solution(mesh):
    finer = Mesh(mesh.devices.reshape(8, 2, 2, 2, 8), SEQ + ("chan",))
    return jax.shard_map(
        body,
        mesh=finer,
        in_specs=(
            P(SEQ, "chan"),
            P(SEQ, "chan"),
            P(SEQ, "chan"),
            P(None, "chan"),
            P(None, "chan"),
            P("chan"),
            P("chan", SEQ),
        ),
        out_specs=P(SEQ, "chan"),
        check_vma=False,
    )
```

```python
import jax
import jax.numpy as jnp
from jax import lax
from jax.experimental import pallas as pl
from jax.experimental.pallas import tpu as pltpu
from jax.sharding import Mesh
from jax.sharding import PartitionSpec as P

F32 = jnp.float32
BF16 = jnp.bfloat16
SEQ = ("z", "xh", "xl", "core")
LANES = 128
VMEM = pl.BlockSpec(memory_space=pltpu.VMEM)
PARAMS = pltpu.CompilerParams(vmem_limit_bytes=48 * 1024 * 1024)


def tile_rows():
    return lax.broadcasted_iota(jnp.int32, (8, LANES), 0).astype(F32)


def chunk_kernel(
    inputs_ref, rate_ref, residue_ref, skip_ref,
    base_ref, before_ref, send_ref, amp_ref, copy_ref, signal_ref, state_ref,
):
    blocks, rows, width = base_ref.shape
    modes = rate_ref.shape[0]
    tiles = rows // 8
    cores = inputs_ref.shape[0]
    first_col = lax.axis_index("core") * width

    def slab(index, carry):
        cols = pl.ds(pl.multiple_of(index * LANES, LANES), LANES)
        source = pl.ds(pl.multiple_of(first_col + index * LANES, LANES), LANES)
        for i in range(blocks):
            key = inputs_ref[i % cores, i // cores, 0, :, source].astype(F32)
            signal_ref[i] = key * inputs_ref[i % cores, i // cores, 1, :, source].astype(F32)
        rate = rate_ref[:, source]
        amp = residue_ref[:, source] * jnp.sqrt(1.0 - jnp.exp(-2.0 * rate))
        amp_ref[:, cols] = amp
        copy_ref[:, cols] = rate
        steps = [jnp.exp(-8.0 * j * rate) for j in range(tiles)]
        scaled = [amp * step for step in steps]
        first = tile_rows()
        taps = [jnp.zeros((8, LANES), F32) for _ in range(tiles)]
        for m in range(modes):
            ahead = jnp.exp(-rate[m : m + 1] * first)
            behind = jnp.exp(-rate[m : m + 1] * (7.0 - first))
            held = [jnp.zeros((8, LANES), F32) for _ in range(blocks)]
            for j in range(tiles):
                taps[j] = taps[j] + scaled[j][m : m + 1] * ahead
                step = steps[tiles - 1 - j][m : m + 1]
                for i in range(blocks):
                    held[i] = held[i] + step * signal_ref[i, 8 * j : 8 * j + 8]
            for i in range(blocks):
                state_ref[i, m : m + 1] = jnp.sum(held[i] * behind, axis=0, keepdims=True)
        decay = jnp.exp(-float(rows) * rate)
        running = jnp.zeros((modes, LANES), F32)
        for i in range(blocks):
            before_ref[i, :, cols] = running
            running = decay * running + state_ref[i]
        send_ref[:, cols] = running
        row_ids = lax.broadcasted_iota(jnp.int32, (rows, LANES), 0)
        skip = skip_ref[0:1, source]

        def block(i, inner):
            signal = signal_ref[i]
            totals = [skip * signal[8 * j : 8 * j + 8] for j in range(tiles)]
            for lag in range(8):
                moved = signal
                if lag:
                    moved = jnp.where(row_ids >= lag, pltpu.roll(signal, lag, 0), 0.0)
                for j in range(tiles):
                    tap = taps[j][lag : lag + 1]
                    for k in range(j, tiles):
                        totals[k] = totals[k] + tap * moved[8 * (k - j) : 8 * (k - j) + 8]
            for j in range(tiles):
                base_ref[i, 8 * j : 8 * j + 8, cols] = totals[j]
            return inner

        return lax.fori_loop(0, blocks, block, carry)

    lax.fori_loop(0, width // LANES, slab, 0)


def total_kernel(length, states_ref, rate_ref, total_ref):
    decay = jnp.exp(-float(length) * rate_ref[...])
    total = states_ref[0]
    for i in range(1, states_ref.shape[0]):
        total = decay * total + states_ref[i]
    for copy in range(total_ref.shape[0]):
        total_ref[copy] = total


def gate_kernel(
    totals_ref, states_ref, before_ref, rate_ref, amp_ref, base_ref, inputs_ref, gated_ref
):
    blocks, rows, width = base_ref.shape
    modes = rate_ref.shape[0]
    tiles = rows // 8
    cores = inputs_ref.shape[0]
    own_z = lax.axis_index("z")
    own_high = lax.axis_index("xh")
    first_col = lax.axis_index("core") * width
    highs = states_ref.shape[0]

    def slab(index, carry):
        cols = pl.ds(pl.multiple_of(index * LANES, LANES), LANES)
        source = pl.ds(pl.multiple_of(first_col + index * LANES, LANES), LANES)
        rate = rate_ref[:, cols]
        amp = amp_ref[:, cols]
        decay = jnp.exp(-float(rows * blocks * highs) * rate)
        running = jnp.zeros((modes, LANES), F32)
        entering = jnp.zeros((modes, LANES), F32)
        for z in range(totals_ref.shape[0]):
            entering = jnp.where(own_z == z, running, entering)
            running = decay * running + totals_ref[z, :, cols]
        decay = jnp.exp(-float(rows * blocks) * rate)
        running = entering
        for high in range(1, highs):
            running = decay * running + states_ref[high - 1, :, cols]
            entering = jnp.where(own_high == high, running, entering)
        steps = [jnp.exp(-8.0 * j * rate) for j in range(tiles)]
        first = tile_rows() + 1.0
        aheads = [jnp.exp(-rate[m : m + 1] * first) for m in range(modes)]
        state = entering
        for i in range(blocks):
            full = (before_ref[i, :, cols] + state) * amp
            if i < blocks - 1:
                state = state * jnp.exp(-float(rows) * rate)
            parts = []
            for j in range(tiles):
                part = base_ref[i, 8 * j : 8 * j + 8, cols]
                scaled = full * steps[j]
                for m in range(modes):
                    part = part + scaled[m : m + 1] * aheads[m]
                parts.append(part)
            gate = inputs_ref[i % cores, i // cores, 2, :, source].astype(F32)
            gated_ref[i, :, cols] = (gate * jnp.concatenate(parts, axis=0)).astype(BF16)
        return carry

    lax.fori_loop(0, width // LANES, slab, 0)


def project_kernel(gated_ref, near_ref, far_ref, last_ref, out_ref):
    cores, shared, rows, half = gated_ref.shape
    gated = [gated_ref[core].reshape(shared * rows, half) for core in range(cores)]
    for j in range(out_ref.shape[1]):
        ref, k = (far_ref, j) if j < far_ref.shape[0] else (last_ref, j - far_ref.shape[0])
        total = 0.0
        for core in range(cores):
            depth = slice(core * half, (core + 1) * half)
            weight = jnp.concatenate([near_ref[j, :, depth], ref[k, :, depth]], axis=0)
            total = total + lax.dot_general(
                gated[core], weight, (((1,), (1,)), ((), ())), preferred_element_type=F32
            )
        out_ref[:, j] = total.astype(BF16).reshape(shared, rows, -1)


def sum_kernel(parts_ref, out_ref):
    low, cores, groups, rows, width = parts_ref.shape
    own_high = lax.axis_index("xh")
    unit = width // 2
    for x_low in range(low):
        totals = []
        for core in range(cores):
            total = parts_ref[x_low, core, 0].astype(F32)
            for j in range(1, groups):
                total = total + parts_ref[x_low, core, j].astype(F32)
            totals.append(total)
        near = [total[:, :unit] for total in totals]
        far = [total[:, unit:] for total in totals]
        near, far = jnp.concatenate(near, axis=1), jnp.concatenate(far, axis=1)
        for high in range(2):
            place = (high * low + x_low) * (cores * unit)
            columns = jnp.where(own_high == high, near, far)
            out_ref[:, place : place + cores * unit] = columns.astype(BF16)


def exchange(x, axes):
    return lax.all_to_all(x, axes, 0, 0, tiled=True)


def body(gate_input, key_input, value_input, decay_rate, residue, skip_gain, out_weight):
    rows, width = key_input.shape
    modes = decay_rate.shape[0]
    z_size, high_size, low_size, cores = (lax.axis_size(a) for a in SEQ)
    y_size = lax.axis_size("chan")
    out_cols = out_weight.shape[1]
    blocks = low_size * cores
    half = width // cores
    own_weight = jnp.broadcast_to(out_weight.T[None], (z_size, out_cols, width))
    near = exchange(own_weight, "z")
    inputs = jnp.stack([key_input, value_input, gate_input])
    inputs = lax.all_gather(lax.all_gather(inputs, "xl"), "core")
    base, before, state, amplitude, rate = pl.pallas_call(
        chunk_kernel,
        out_shape=(
            jax.ShapeDtypeStruct((blocks, rows, half), F32),
            jax.ShapeDtypeStruct((blocks, modes, half), F32),
            jax.ShapeDtypeStruct((modes, half), F32),
            jax.ShapeDtypeStruct((modes, half), F32),
            jax.ShapeDtypeStruct((modes, half), F32),
        ),
        in_specs=[VMEM] * 4,
        out_specs=(VMEM,) * 5,
        scratch_shapes=[
            pltpu.VMEM((blocks, rows, LANES), F32),
            pltpu.VMEM((blocks, modes, LANES), F32),
        ],
        compiler_params=PARAMS,
        name="chunk",
    )(inputs, decay_rate, residue, skip_gain[None, :])
    states = lax.all_gather(state, "xh")
    total = pl.pallas_call(
        lambda *refs: total_kernel(rows * blocks, *refs),
        out_shape=jax.ShapeDtypeStruct((z_size, modes, half), F32),
        in_specs=[VMEM] * 2,
        out_specs=VMEM,
        compiler_params=PARAMS,
        name="total",
    )(states, rate)
    total, near = lax.optimization_barrier((total, near))
    far = [
        lax.ppermute(part, "xh", [(0, 1), (1, 0)]) for part in jnp.split(near, 2, axis=0)
    ]
    totals = exchange(total, "z")
    gated = pl.pallas_call(
        gate_kernel,
        out_shape=jax.ShapeDtypeStruct((blocks, rows, half), BF16),
        in_specs=[VMEM] * 7,
        out_specs=VMEM,
        compiler_params=PARAMS,
        name="gate",
    )(totals, states, before, rate, amplitude, base, inputs)
    gated = lax.all_gather(gated, "core")
    piece = (rows, high_size * out_cols)
    parts = pl.pallas_call(
        project_kernel,
        out_shape=jax.ShapeDtypeStruct((blocks, y_size) + piece, BF16),
        in_specs=[VMEM] * 4,
        out_specs=VMEM,
        compiler_params=PARAMS,
        name="project",
    )(gated, near, *far)
    parts = exchange(parts.reshape((y_size * blocks,) + piece), ("xl", "core", "chan"))
    return pl.pallas_call(
        sum_kernel,
        out_shape=jax.ShapeDtypeStruct((rows, width), BF16),
        in_specs=[VMEM],
        out_specs=VMEM,
        compiler_params=PARAMS,
        name="sum_parts",
    )(parts.reshape((low_size, cores, y_size) + piece))


def solution(mesh):
    finer = Mesh(mesh.devices.reshape(8, 2, 2, 2, 8), SEQ + ("chan",))
    return jax.shard_map(
        body,
        mesh=finer,
        in_specs=(
            P(SEQ, "chan"),
            P(SEQ, "chan"),
            P(SEQ, "chan"),
            P(None, "chan"),
            P(None, "chan"),
            P("chan"),
            P("chan", SEQ),
        ),
        out_specs=P(SEQ, "chan"),
        check_vma=False,
    )
```

```python
import jax
import jax.numpy as jnp
from jax import lax
from jax.experimental import pallas as pl
from jax.experimental.pallas import tpu as pltpu
from jax.sharding import Mesh
from jax.sharding import PartitionSpec as P

F32 = jnp.float32
BF16 = jnp.bfloat16
SEQ = ("z", "xh", "xl", "core")
LANES = 128
VMEM = pl.BlockSpec(memory_space=pltpu.VMEM)
PARAMS = pltpu.CompilerParams(vmem_limit_bytes=48 * 1024 * 1024)


def tile_rows():
    return lax.broadcasted_iota(jnp.int32, (8, LANES), 0).astype(F32)


def chunk_kernel(
    inputs_ref, filters_ref,
    base_ref, before_ref, send_ref, amp_ref, copy_ref, signal_ref, state_ref,
):
    blocks, rows, width = base_ref.shape
    modes = amp_ref.shape[0]
    tiles = rows // 8
    cores = inputs_ref.shape[0]
    first_col = lax.axis_index("core") * width

    def slab(index, carry):
        cols = pl.ds(pl.multiple_of(index * LANES, LANES), LANES)
        source = pl.ds(pl.multiple_of(first_col + index * LANES, LANES), LANES)
        for i in range(blocks):
            key = inputs_ref[i % cores, i // cores, 0, :, source].astype(F32)
            signal_ref[i] = key * inputs_ref[i % cores, i // cores, 1, :, source].astype(F32)
        rate = filters_ref[:modes, source]
        amp = filters_ref[modes : 2 * modes, source] * jnp.sqrt(1.0 - jnp.exp(-2.0 * rate))
        amp_ref[:, cols] = amp
        copy_ref[:, cols] = rate
        steps = [jnp.exp(-8.0 * j * rate) for j in range(tiles)]
        scaled = [amp * step for step in steps]
        first = tile_rows()
        taps = [jnp.zeros((8, LANES), F32) for _ in range(tiles)]
        for m in range(modes):
            ahead = jnp.exp(-rate[m : m + 1] * first)
            behind = jnp.exp(-rate[m : m + 1] * (7.0 - first))
            held = [jnp.zeros((8, LANES), F32) for _ in range(blocks)]
            for j in range(tiles):
                taps[j] = taps[j] + scaled[j][m : m + 1] * ahead
                step = steps[tiles - 1 - j][m : m + 1]
                for i in range(blocks):
                    held[i] = held[i] + step * signal_ref[i, 8 * j : 8 * j + 8]
            for i in range(blocks):
                state_ref[i, m : m + 1] = jnp.sum(held[i] * behind, axis=0, keepdims=True)
        decay = jnp.exp(-float(rows) * rate)
        running = jnp.zeros((modes, LANES), F32)
        for i in range(blocks):
            before_ref[i, :, cols] = running
            running = decay * running + state_ref[i]
        send_ref[:, cols] = running
        row_ids = lax.broadcasted_iota(jnp.int32, (rows, LANES), 0)
        skip = filters_ref[2 * modes : 2 * modes + 1, source]

        def block(i, inner):
            signal = signal_ref[i]
            totals = [skip * signal[8 * j : 8 * j + 8] for j in range(tiles)]
            for lag in range(8):
                moved = signal
                if lag:
                    moved = jnp.where(row_ids >= lag, pltpu.roll(signal, lag, 0), 0.0)
                for j in range(tiles):
                    tap = taps[j][lag : lag + 1]
                    for k in range(j, tiles):
                        totals[k] = totals[k] + tap * moved[8 * (k - j) : 8 * (k - j) + 8]
            for j in range(tiles):
                base_ref[i, 8 * j : 8 * j + 8, cols] = totals[j]
            return inner

        return lax.fori_loop(0, blocks, block, carry)

    lax.fori_loop(0, width // LANES, slab, 0)


def total_kernel(length, states_ref, rate_ref, total_ref):
    decay = jnp.exp(-float(length) * rate_ref[...])
    total = states_ref[0]
    for i in range(1, states_ref.shape[0]):
        total = decay * total + states_ref[i]
    for copy in range(total_ref.shape[0]):
        total_ref[copy] = total


def gate_kernel(
    totals_ref, states_ref, before_ref, rate_ref, amp_ref, base_ref, inputs_ref, gated_ref
):
    blocks, rows, width = base_ref.shape
    modes = rate_ref.shape[0]
    tiles = rows // 8
    cores = inputs_ref.shape[0]
    own_z = lax.axis_index("z")
    own_high = lax.axis_index("xh")
    first_col = lax.axis_index("core") * width
    highs = states_ref.shape[0]

    def slab(index, carry):
        cols = pl.ds(pl.multiple_of(index * LANES, LANES), LANES)
        source = pl.ds(pl.multiple_of(first_col + index * LANES, LANES), LANES)
        rate = rate_ref[:, cols]
        amp = amp_ref[:, cols]
        decay = jnp.exp(-float(rows * blocks * highs) * rate)
        running = jnp.zeros((modes, LANES), F32)
        entering = jnp.zeros((modes, LANES), F32)
        for z in range(totals_ref.shape[0]):
            entering = jnp.where(own_z == z, running, entering)
            running = decay * running + totals_ref[z, :, cols]
        decay = jnp.exp(-float(rows * blocks) * rate)
        running = entering
        for high in range(1, highs):
            running = decay * running + states_ref[high - 1, :, cols]
            entering = jnp.where(own_high == high, running, entering)
        steps = [jnp.exp(-8.0 * j * rate) for j in range(tiles)]
        first = tile_rows() + 1.0
        aheads = [jnp.exp(-rate[m : m + 1] * first) for m in range(modes)]
        state = entering
        for i in range(blocks):
            full = (before_ref[i, :, cols] + state) * amp
            if i < blocks - 1:
                state = state * jnp.exp(-float(rows) * rate)
            parts = []
            for j in range(tiles):
                part = base_ref[i, 8 * j : 8 * j + 8, cols]
                scaled = full * steps[j]
                for m in range(modes):
                    part = part + scaled[m : m + 1] * aheads[m]
                parts.append(part)
            gate = inputs_ref[i % cores, i // cores, 2, :, source].astype(F32)
            gated_ref[i, :, cols] = (gate * jnp.concatenate(parts, axis=0)).astype(BF16)
        return carry

    lax.fori_loop(0, width // LANES, slab, 0)


def project_kernel(gated_ref, near_ref, far_ref, out_ref):
    cores, shared, rows, half = gated_ref.shape
    gated = [gated_ref[core].reshape(shared * rows, half) for core in range(cores)]
    for j in range(out_ref.shape[1]):
        total = 0.0
        for core in range(cores):
            depth = slice(core * half, (core + 1) * half)
            weight = jnp.concatenate([near_ref[j, :, depth], far_ref[j, :, depth]], axis=0)
            total = total + lax.dot_general(
                gated[core], weight, (((1,), (1,)), ((), ())), preferred_element_type=F32
            )
        out_ref[:, j] = total.astype(BF16).reshape(shared, rows, -1)


def sum_kernel(parts_ref, out_ref):
    low, cores, groups, rows, width = parts_ref.shape
    own_high = lax.axis_index("xh")
    unit = width // 2
    for x_low in range(low):
        totals = []
        for core in range(cores):
            total = parts_ref[x_low, core, 0].astype(F32)
            for j in range(1, groups):
                total = total + parts_ref[x_low, core, j].astype(F32)
            totals.append(total)
        near = [total[:, :unit] for total in totals]
        far = [total[:, unit:] for total in totals]
        near, far = jnp.concatenate(near, axis=1), jnp.concatenate(far, axis=1)
        for high in range(2):
            place = (high * low + x_low) * (cores * unit)
            columns = jnp.where(own_high == high, near, far)
            out_ref[:, place : place + cores * unit] = columns.astype(BF16)


def exchange(x, axes):
    return lax.all_to_all(x, axes, 0, 0, tiled=True)


def body(gate_input, key_input, value_input, decay_rate, residue, skip_gain, out_weight):
    rows, width = key_input.shape
    modes = decay_rate.shape[0]
    z_size, high_size, low_size, cores = (lax.axis_size(a) for a in SEQ)
    y_size = lax.axis_size("chan")
    out_cols = out_weight.shape[1]
    blocks = low_size * cores
    half = width // cores
    own_weight = jnp.broadcast_to(out_weight.T[None], (z_size, out_cols, width))
    near = exchange(own_weight, "z")
    inputs = jnp.stack([key_input, value_input, gate_input])
    filters = jnp.concatenate([decay_rate, residue, skip_gain[None, :]], axis=0)
    inputs, filters = lax.optimization_barrier((inputs, filters))
    inputs = lax.all_gather(lax.all_gather(inputs, "xl"), "core")
    base, before, state, amplitude, rate = pl.pallas_call(
        chunk_kernel,
        out_shape=(
            jax.ShapeDtypeStruct((blocks, rows, half), F32),
            jax.ShapeDtypeStruct((blocks, modes, half), F32),
            jax.ShapeDtypeStruct((modes, half), F32),
            jax.ShapeDtypeStruct((modes, half), F32),
            jax.ShapeDtypeStruct((modes, half), F32),
        ),
        in_specs=[VMEM] * 2,
        out_specs=(VMEM,) * 5,
        scratch_shapes=[
            pltpu.VMEM((blocks, rows, LANES), F32),
            pltpu.VMEM((blocks, modes, LANES), F32),
        ],
        compiler_params=PARAMS,
        name="chunk",
    )(inputs, filters)
    states = lax.all_gather(state, "xh")
    total = pl.pallas_call(
        lambda *refs: total_kernel(rows * blocks, *refs),
        out_shape=jax.ShapeDtypeStruct((z_size, modes, half), F32),
        in_specs=[VMEM] * 2,
        out_specs=VMEM,
        compiler_params=PARAMS,
        name="total",
    )(states, rate)
    total, near = lax.optimization_barrier((total, near))
    far = lax.ppermute(near, "xh", [(0, 1), (1, 0)])
    totals = exchange(total, "z")
    gated = pl.pallas_call(
        gate_kernel,
        out_shape=jax.ShapeDtypeStruct((blocks, rows, half), BF16),
        in_specs=[VMEM] * 7,
        out_specs=VMEM,
        compiler_params=PARAMS,
        name="gate",
    )(totals, states, before, rate, amplitude, base, inputs)
    gated = lax.all_gather(gated, "core")
    piece = (rows, high_size * out_cols)
    parts = pl.pallas_call(
        project_kernel,
        out_shape=jax.ShapeDtypeStruct((blocks, y_size) + piece, BF16),
        in_specs=[VMEM] * 3,
        out_specs=VMEM,
        compiler_params=PARAMS,
        name="project",
    )(gated, near, far)
    parts = exchange(parts.reshape((y_size * blocks,) + piece), ("xl", "core", "chan"))
    return pl.pallas_call(
        sum_kernel,
        out_shape=jax.ShapeDtypeStruct((rows, width), BF16),
        in_specs=[VMEM],
        out_specs=VMEM,
        compiler_params=PARAMS,
        name="sum_parts",
    )(parts.reshape((low_size, cores, y_size) + piece))


def solution(mesh):
    finer = Mesh(mesh.devices.reshape(8, 2, 2, 2, 8), SEQ + ("chan",))
    return jax.shard_map(
        body,
        mesh=finer,
        in_specs=(
            P(SEQ, "chan"),
            P(SEQ, "chan"),
            P(SEQ, "chan"),
            P(None, "chan"),
            P(None, "chan"),
            P("chan"),
            P("chan", SEQ),
        ),
        out_specs=P(SEQ, "chan"),
        check_vma=False,
    )
```
